32 devices in a mesh: grp: 4 (over x, core), shard: 8 (over z, y).
Axes of the slice: x: 2, y: 2, z: 4, core: 2. Of those that a mesh axis runs over, the one named last changes fastest.
Arguments:
- query_states: bfloat16 [8192, 512], P(('grp', 'shard')), may hold values from -7.5 to 7.5
- key_states: bfloat16 [8192, 512], P(('grp', 'shard')), may hold values from -7.5 to 7.5
- value_states: bfloat16 [8192, 512], P(('grp', 'shard')), may hold values from -7.5 to 7.5
- valid_mask: int32 [8192], P(('grp', 'shard')), may hold values from 0 to 1, as said below
- attended_grad: bfloat16 [8192, 512], P(('grp', 'shard')), may hold values from -7.5 to 7.5
Outputs:
- attended: bfloat16 [8192, 512], P(('grp', 'shard'))
- query_grad: bfloat16 [8192, 512], P(('grp', 'shard'))
- key_grad: bfloat16 [8192, 512], P(('grp', 'shard'))
- value_grad: bfloat16 [8192, 512], P(('grp', 'shard'))
The draws below stay inside these ranges and needn't reach their ends.
Inputs may be any that keep to these rules, and one draw needn't show every extreme that they name: `valid_mask`: in each device's run of 256 positions the ones form a prefix of 64 to 256 positions; the first run is all ones and the last has exactly 64.
All inputs are finite; a program needn't handle non-finite values.
Results may differ from the reference program's by a relative error of at most 0.0055.
Values may be sent and summed in bfloat16 or wider, within the bound.
A program may use at most 128 MiB of HBM per device.

```python
import jax
import jax.numpy as jnp
from jax import lax

HEADS = 4
HEAD_DIM = 128
WIDTH = 512
BLOCK = 128
COARSE = 64
TOK_DEV = 256
LEVELS = 5
TOKENS = 8192


LIMIT = 7.5


def session_table(key, amp):
    seg_len = max(TOKENS // (4 * COARSE), 1)
    table = jax.random.normal(key, (TOKENS // seg_len, WIDTH), jnp.float32) * amp
    return jnp.repeat(table, seg_len, axis=0)


def draw_query_states(key, part):
    rough = jnp.clip(jax.random.normal(jax.random.fold_in(key, 11), (TOKENS, WIDTH), jnp.float32), -LIMIT, LIMIT)
    return rough.astype(jnp.bfloat16)


def draw_key_states(key, part):
    rough = 0.8 * jax.random.normal(jax.random.fold_in(key, 21), (TOKENS, WIDTH), jnp.float32) + session_table(jax.random.fold_in(key, 22), 0.6)
    rough = jnp.clip(rough, -LIMIT, LIMIT)
    return rough.astype(jnp.bfloat16)


def draw_value_states(key, part):
    rough = 0.8 * jax.random.normal(jax.random.fold_in(key, 31), (TOKENS, WIDTH), jnp.float32) + session_table(jax.random.fold_in(key, 32), 0.6)
    return jnp.clip(rough, -LIMIT, LIMIT).astype(jnp.bfloat16)


def draw_attended_grad(key, part):
    common = jax.random.normal(jax.random.fold_in(key, 45), (1, WIDTH), jnp.float32)
    rough = 0.7 * jax.random.normal(jax.random.fold_in(key, 41), (TOKENS, WIDTH), jnp.float32)
    rough = rough + session_table(jax.random.fold_in(key, 44), 0.5) + 0.5 * common
    return jnp.clip(rough, -LIMIT, LIMIT).astype(jnp.bfloat16)


def draw_valid_mask(key, part):
    device_count = TOKENS // TOK_DEV
    lengths = jax.random.randint(jax.random.fold_in(key, 51), (device_count,), TOK_DEV // 4, TOK_DEV + 1)
    lengths = lengths.at[0].set(TOK_DEV).at[device_count - 1].set(TOK_DEV // 4)
    positions = jnp.arange(TOK_DEV, dtype=jnp.int32)
    return (positions[None, :] < lengths[:, None]).astype(jnp.int32).reshape(TOKENS)


def setup_inputs(seed: int = 0) -> dict:
    seeds = jax.random.split(jax.random.key(seed), 6)
    query_states = draw_query_states(jax.random.fold_in(seeds[5], 71), 0)
    key_states = draw_key_states(jax.random.fold_in(seeds[5], 71), 0)
    value_states = draw_value_states(jax.random.fold_in(seeds[5], 71), 0)
    valid_mask = draw_valid_mask(jax.random.fold_in(seeds[5], 71), 0)
    attended_grad = draw_attended_grad(jax.random.fold_in(seeds[5], 71), 0)
    return dict(query_states=query_states, key_states=key_states, value_states=value_states, valid_mask=valid_mask, attended_grad=attended_grad)


MASKED = -1.0e30


def flip_pairs(array):
    shape = array.shape
    paired = array.reshape((shape[0] // 2, 2) + shape[1:])
    return jnp.flip(paired, axis=1).reshape(shape)


def reference(query_states, key_states, value_states, valid_mask, attended_grad):
    feat_width = query_states.shape[1]
    score_scale = HEAD_DIM ** -0.5
    mask_float = valid_mask.astype(jnp.float32)
    kv_states = jnp.stack([key_states, value_states], axis=1)
    sib_means = []
    sib_live = []
    count_tables = []
    for lvl in range(LEVELS):
        group_size = (BLOCK * 2 ** (lvl + 1)) // COARSE
        row_count = TOKENS // group_size
        group_sums = jnp.sum(kv_states.reshape(row_count, group_size, 2, feat_width).astype(jnp.float32) * mask_float.reshape(row_count, group_size, 1, 1), axis=1)
        group_count = jnp.sum(mask_float.reshape(row_count, group_size), axis=1)
        group_means = (group_sums / jnp.maximum(group_count, 1.0)[:, None, None]).astype(jnp.bfloat16)
        span_count = row_count // COARSE
        sib_means.append(flip_pairs(group_means.reshape(span_count, COARSE, 2, feat_width)))
        sib_live.append(flip_pairs(group_count.reshape(span_count, COARSE)) > 0)
        count_tables.append(group_count.reshape(span_count, COARSE))
    span_len = 2 * BLOCK
    nspans = TOKENS // span_len
    far_rows = LEVELS * COARSE
    padded_kv = jnp.pad(kv_states, ((BLOCK, BLOCK), (0, 0), (0, 0)))
    padded_mask = jnp.pad(mask_float, (BLOCK, BLOCK))
    near_init = jnp.zeros((TOKENS + 2 * BLOCK, 2, feat_width), jnp.float32)
    grad_init = tuple(jnp.zeros(table.shape, jnp.float32) for table in sib_means)

    def step(state_carry, span_index):
        near_acc, grad_acc = state_carry
        row_start = span_index * span_len
        query_span = lax.dynamic_slice_in_dim(query_states, row_start, span_len, 0).astype(jnp.float32).reshape(2, BLOCK, HEADS, HEAD_DIM)
        cot_span = lax.dynamic_slice_in_dim(attended_grad, row_start, span_len, 0).astype(jnp.float32).reshape(2, BLOCK, HEADS, HEAD_DIM)
        window = lax.dynamic_slice_in_dim(padded_kv, row_start, 4 * BLOCK, 0)
        window_mask = lax.dynamic_slice_in_dim(padded_mask, row_start, 4 * BLOCK, 0)
        near_kv = jnp.stack([window[:3 * BLOCK], window[BLOCK:]], axis=0).astype(jnp.float32)
        near_mask = jnp.stack([window_mask[:3 * BLOCK], window_mask[BLOCK:]], axis=0)
        near_keys = near_kv[:, :, 0].reshape(2, 3 * BLOCK, HEADS, HEAD_DIM)
        near_vals = near_kv[:, :, 1].reshape(2, 3 * BLOCK, HEADS, HEAD_DIM)
        far_kv = jnp.concatenate([lax.dynamic_index_in_dim(sib_means[lvl], span_index // (2 ** lvl), 0, keepdims=False) for lvl in range(LEVELS)], axis=0).astype(jnp.float32)
        far_ok = jnp.concatenate([lax.dynamic_index_in_dim(sib_live[lvl], span_index // (2 ** lvl), 0, keepdims=False) for lvl in range(LEVELS)], axis=0)
        far_keys = far_kv[:, 0].reshape(far_rows, HEADS, HEAD_DIM)
        far_vals = far_kv[:, 1].reshape(far_rows, HEADS, HEAD_DIM)
        near_score = jnp.einsum("bqhd,bkhd->bqhk", query_span, near_keys) * score_scale
        near_score = jnp.where(near_mask[:, None, None, :] > 0, near_score, MASKED)
        far_score = jnp.einsum("bqhd,khd->bqhk", query_span, far_keys) * score_scale
        far_score = jnp.where(far_ok[None, None, None, :], far_score, MASKED)
        row_max = jnp.maximum(jnp.max(near_score, axis=-1), jnp.max(far_score, axis=-1))
        near_exp = jnp.exp(near_score - row_max[..., None])
        far_exp = jnp.exp(far_score - row_max[..., None])
        row_total = jnp.sum(near_exp, axis=-1) + jnp.sum(far_exp, axis=-1)
        near_prob = near_exp / row_total[..., None]
        far_prob = far_exp / row_total[..., None]
        nearby_half_rows = lax.optimization_barrier(near_prob.astype(jnp.bfloat16)).astype(jnp.float32)
        far_half = lax.optimization_barrier(far_prob.astype(jnp.bfloat16)).astype(jnp.float32)
        attended_span = jnp.einsum("bqhk,bkhd->bqhd", nearby_half_rows, near_vals) + jnp.einsum("bqhk,khd->bqhd", far_half, far_vals)
        near_dp = jnp.einsum("bqhd,bkhd->bqhk", cot_span, near_vals)
        far_dp = jnp.einsum("bqhd,khd->bqhk", cot_span, far_vals)
        row_delta = jnp.sum(near_prob * near_dp, axis=-1) + jnp.sum(far_prob * far_dp, axis=-1)
        nearby_delta_score = lax.optimization_barrier((near_prob * (near_dp - row_delta[..., None])).astype(jnp.bfloat16)).astype(jnp.float32)
        far_ds = lax.optimization_barrier((far_prob * (far_dp - row_delta[..., None])).astype(jnp.bfloat16)).astype(jnp.float32)
        query_span_grad = score_scale * (jnp.einsum("bqhk,bkhd->bqhd", nearby_delta_score, near_keys) + jnp.einsum("bqhk,khd->bqhd", far_ds, far_keys))
        near_gk = score_scale * jnp.einsum("bqhk,bqhd->bkhd", nearby_delta_score, query_span)
        near_gv = jnp.einsum("bqhk,bqhd->bkhd", nearby_half_rows, cot_span)
        near_grad = jnp.stack([near_gk.reshape(2, 3 * BLOCK, feat_width), near_gv.reshape(2, 3 * BLOCK, feat_width)], axis=2)
        window_grad = jnp.zeros((4 * BLOCK, 2, feat_width), jnp.float32)
        window_grad = window_grad.at[:3 * BLOCK].add(near_grad[0]).at[BLOCK:].add(near_grad[1])
        old_rows = lax.dynamic_slice_in_dim(near_acc, row_start, 4 * BLOCK, 0)
        near_acc = lax.dynamic_update_slice_in_dim(near_acc, old_rows + window_grad, row_start, 0)
        far_gk = score_scale * jnp.einsum("bqhk,bqhd->khd", far_ds, query_span)
        far_gv = jnp.einsum("bqhk,bqhd->khd", far_half, cot_span)
        far_grad = jnp.stack([far_gk.reshape(far_rows, feat_width), far_gv.reshape(far_rows, feat_width)], axis=1)
        new_acc = []
        for lvl in range(LEVELS):
            position = span_index // (2 ** lvl)
            piece = far_grad[lvl * COARSE:(lvl + 1) * COARSE]
            old_tile = lax.dynamic_index_in_dim(grad_acc[lvl], position, 0, keepdims=False)
            new_acc.append(lax.dynamic_update_index_in_dim(grad_acc[lvl], old_tile + piece, position, 0))
        outputs = (attended_span.reshape(span_len, feat_width).astype(jnp.bfloat16), query_span_grad.reshape(span_len, feat_width).astype(jnp.bfloat16))
        return (near_acc, tuple(new_acc)), outputs

    final_carry, stacked = lax.scan(step, (near_init, grad_init), jnp.arange(nspans, dtype=jnp.int32))
    near_acc, grad_acc = final_carry
    attended = stacked[0].reshape(TOKENS, feat_width)
    query_grad = stacked[1].reshape(TOKENS, feat_width)
    kv_grad = near_acc[BLOCK:BLOCK + TOKENS]
    for lvl in range(LEVELS):
        group_size = (BLOCK * 2 ** (lvl + 1)) // COARSE
        row_count = TOKENS // group_size
        tile_grad = flip_pairs(grad_acc[lvl]) / jnp.maximum(count_tables[lvl], 1.0)[..., None, None]
        spread = tile_grad.reshape(row_count, 1, 2, feat_width) * mask_float.reshape(row_count, group_size, 1, 1)
        kv_grad = kv_grad + spread.reshape(TOKENS, 2, feat_width)
    return attended, query_grad, kv_grad[:, 0].astype(jnp.bfloat16), kv_grad[:, 1].astype(jnp.bfloat16)
```

```python
import functools

import jax
import jax.numpy as jnp
from jax import lax
from jax.experimental import pallas as pl
from jax.experimental.pallas import tpu as pltpu
from jax.sharding import PartitionSpec as P

HEADS = 4
HEAD_DIM = 128
BLOCK = 128
COARSE = 64
DIRECT = 5
TOK = 256
WIDTH = HEADS * HEAD_DIM
PACK = 2 * HEADS
TILE = PACK * COARSE
SCALE = HEAD_DIM ** (-0.5)
MASKED = -1e30
DEAD = 1024.0
DEAD_SUM = 65536.0
MESH = pl.DeviceIdType.MESH
BF = jnp.bfloat16
F32 = jnp.float32


def rows_of(level):
    return COARSE >> level


def up_offset(level):
    return sum(PACK * rows_of(i) for i in range(level))


def row_offset(level):
    return sum(rows_of(i) for i in range(level))


def iota(shape, dim):
    return lax.broadcasted_iota(jnp.int32, shape, dim)


def dot(a, b, dims):
    return lax.dot_general(a, b, (dims, ((), ())), preferred_element_type=F32)


NN = ((1,), (0,))
NT = ((1,), (1,))
TN = ((0,), (0,))


def regroup(level, inverse):
    rows = rows_of(level)
    big = iota((TILE, TILE), 1 if inverse else 0)
    small = iota((TILE, TILE), 0 if inverse else 1)
    pack = big // COARSE
    row = big % COARSE
    src = (row // rows) * (PACK * rows) + pack * rows + row % rows
    return jnp.where(src == small, 1.0, 0.0).astype(BF)


def level_row_maps(direct, shape, dim):
    idx = iota(shape, dim)
    low = jnp.full(shape, 2 * TOK, jnp.int32)
    size = jnp.ones(shape, jnp.int32)
    for level in range(direct):
        group = 4 << level
        at = row_offset(level)
        inside = (idx >= at) & (idx < at + rows_of(level))
        low = jnp.where(inside, (idx - at) * group, low)
        size = jnp.where(inside, group, size)
    return low, size


def kernel(
    n_grp, n_shard, direct, extra,
    q_ref, k_ref, v_ref, m_ref, c_ref, *rest,
):
    if extra:
        xt_ref, att_ref, qg_ref, kg_ref, vg_ref, xg_ref, *rest = rest
    else:
        att_ref, qg_ref, kg_ref, vg_ref, *rest = rest
    (kn, vn, up, far, ftile, small, s_near, dp_near, own_g, edge_s, edge_r, gtile, gsend,
     grecv, gsum, halo_ss, halo_rs, up_ss, up_rs, ed_ss, ed_rs, dn_ss, dn_rs) = rest
    n_dev = n_grp * n_shard
    me = lax.axis_index("grp") * n_shard + lax.axis_index("shard")
    span = 1 << direct
    far_rows = (direct + extra) * COARSE

    def where_is(dev):
        return (dev // n_shard, dev % n_shard)

    def sibling(level):
        part = me // (1 << level)
        return (part + 1 - 2 * (part % 2)) * (1 << level)

    base = (me // span) * span
    at_low = me == base
    at_high = me == base + span - 1
    has_prev = me > 0
    has_next = me < n_dev - 1
    out_prev = has_prev & at_low
    out_next = has_next & at_high
    barrier = pltpu.get_barrier_semaphore()

    def hello(t, _):
        pl.semaphore_signal(
            barrier, inc=1, device_id=where_is(base + (me - base + t) % span), device_id_type=MESH
        )
        return 0

    lax.fori_loop(1, span, hello, 0)
    if n_dev > span:
        @pl.when(out_prev)
        def _():
            pl.semaphore_signal(barrier, inc=1, device_id=where_is(me - 1), device_id_type=MESH)

        @pl.when(out_next)
        def _():
            pl.semaphore_signal(barrier, inc=1, device_id=where_is(me + 1), device_id_type=MESH)

    count = jnp.sum(m_ref[...], axis=1, keepdims=True)
    live_col = iota((TOK, 1), 0) < count
    kn[BLOCK:BLOCK + TOK, :] = jnp.where(live_col, k_ref[...].astype(F32), DEAD).astype(BF)
    vn[BLOCK:BLOCK + TOK, :] = v_ref[...]
    low, size = level_row_maps(direct, (128, TOK), 0)
    pos = iota((128, TOK), 1)
    pool = jnp.where((pos >= low) & (pos < low + size) & (pos < count), 1.0, 0.0).astype(BF)
    low_c, size_c = level_row_maps(direct, (128, 1), 0)
    row_count = jnp.clip(count - low_c, 0, size_c).astype(F32)
    row_div = jnp.maximum(row_count, 1.0)
    for pack in range(PACK):
        ref = k_ref if pack < HEADS else v_ref
        lane = (pack % HEADS) * HEAD_DIM
        mean = dot(pool, ref[:, lane:lane + HEAD_DIM], NN) / row_div
        if pack < HEADS:
            mean = jnp.where(row_count > 0, mean, DEAD)
        for level in range(direct):
            rows = rows_of(level)
            part = mean[row_offset(level):row_offset(level) + rows]
            if rows >= 16:
                at = up_offset(level) + pack * rows
                up[at:at + rows, :] = part.astype(BF)
            else:
                at = up_offset(level) - up_offset(3) + pack * rows
                small[at:at + rows, :] = part
    if direct > 3:
        tail = up_offset(direct) - up_offset(3)
        up[up_offset(3):up_offset(direct), :] = small[0:tail, :].astype(BF)

    pl.semaphore_wait(barrier, span - 1)
    if n_dev > span:
        @pl.when(out_prev)
        def _():
            pl.semaphore_wait(barrier, 1)

        @pl.when(out_next)
        def _():
            pl.semaphore_wait(barrier, 1)

    def halo(which, side):
        ref = kn if which == 0 else vn
        slot = 2 * which + side
        if side == 0:
            src, dst, dev = ref.at[BLOCK:2 * BLOCK, :], ref.at[3 * BLOCK:4 * BLOCK, :], me - 1
        else:
            src, dst, dev = ref.at[2 * BLOCK:3 * BLOCK, :], ref.at[0:BLOCK, :], me + 1
        return pltpu.make_async_remote_copy(
            src_ref=src, dst_ref=dst, send_sem=halo_ss.at[slot], recv_sem=halo_rs.at[slot],
            device_id=where_is(dev), device_id_type=MESH,
        )

    @pl.when(has_prev)
    def _():
        halo(0, 0).start()
        halo(1, 0).start()

    @pl.when(has_next)
    def _():
        halo(0, 1).start()
        halo(1, 1).start()

    @pl.when(jnp.logical_not(has_prev))
    def _():
        kn[0:BLOCK, :] = jnp.full((BLOCK, WIDTH), DEAD, BF)
        vn[0:BLOCK, :] = jnp.zeros((BLOCK, WIDTH), BF)
        edge_r[0] = jnp.zeros((BLOCK, 2 * WIDTH), BF)

    @pl.when(jnp.logical_not(has_next))
    def _():
        kn[3 * BLOCK:4 * BLOCK, :] = jnp.full((BLOCK, WIDTH), DEAD, BF)
        vn[3 * BLOCK:4 * BLOCK, :] = jnp.zeros((BLOCK, WIDTH), BF)
        edge_r[1] = jnp.zeros((BLOCK, 2 * WIDTH), BF)

    def spread_out(level, source, target, send_sem, recv_sem):
        size = PACK * rows_of(level)
        parts = 1 << level
        to = sibling(level)
        land = pl.multiple_of(level * TILE + (me % parts) * size, size)

        def send(t, _):
            m = (me + t) % parts
            pltpu.make_async_remote_copy(
                src_ref=source(m), dst_ref=target.at[pl.ds(land, size), :],
                send_sem=send_sem.at[level], recv_sem=recv_sem.at[level],
                device_id=where_is(to + m), device_id_type=MESH,
            ).start()
            return 0

        if parts == 1:
            send(0, 0)
        else:
            lax.fori_loop(0, parts, send, 0)

    for level in reversed(range(direct)):
        at = up_offset(level)
        spread_out(
            level, lambda m, at=at, n=PACK * rows_of(level): up.at[at:at + n, :], far, up_ss, up_rs
        )

    @pl.when(has_next)
    def _():
        halo(0, 0).wait_recv()
        halo(1, 0).wait_recv()

    @pl.when(has_prev)
    def _():
        halo(0, 1).wait_recv()
        halo(1, 1).wait_recv()

    ones = jnp.ones((8, HEAD_DIM), BF)
    block_row = iota((TOK, 1), 0) // BLOCK
    block_col = iota((1, 4 * BLOCK), 1) // BLOCK
    window = (block_col >= block_row) & (block_col <= block_row + 2)
    for head in range(HEADS):
        lane = slice(head * HEAD_DIM, (head + 1) * HEAD_DIM)
        k = kn[:, lane]
        ok = window & (dot(ones, k, NT)[0:1] < DEAD_SUM)
        s_near[head] = jnp.where(ok, dot(q_ref[:, lane], k, NT) * SCALE, MASKED)
        dp_near[head] = dot(c_ref[:, lane], vn[:, lane], NT)

    for level in range(direct):
        whole = far.at[level * TILE:(level + 1) * TILE, :]
        pltpu.make_async_copy(whole, whole, up_rs.at[level]).wait()
        rows = rows_of(level)
        if level == 0:
            ftile[0] = whole[...]
        elif rows >= 16:
            for m in range(1 << level):
                for pack in range(PACK):
                    src = m * PACK * rows + pack * rows
                    dst = pack * COARSE + m * rows
                    ftile[level, dst:dst + rows, :] = far[
                        level * TILE + src:level * TILE + src + rows, :]
        else:
            ftile[level] = dot(regroup(level, False), whole[...], NN).astype(BF)
    for e in range(extra):
        ftile[direct + e] = xt_ref[e]

    for head in range(HEADS):
        lane = slice(head * HEAD_DIM, (head + 1) * HEAD_DIM)
        k_at = head * COARSE
        v_at = (HEADS + head) * COARSE
        fk = jnp.concatenate([ftile[i, k_at:k_at + COARSE, :] for i in range(direct + extra)], 0)
        fv = jnp.concatenate([ftile[i, v_at:v_at + COARSE, :] for i in range(direct + extra)], 0)
        q = q_ref[:, lane]
        c = c_ref[:, lane]
        ok = dot(ones, fk, NT)[0:1] < DEAD_SUM
        s_f = jnp.where(ok, dot(q, fk, NT) * SCALE, MASKED)
        dp_f = dot(c, fv, NT)
        s_n = s_near[head]
        dp_n = dp_near[head]
        top = jnp.maximum(jnp.max(s_n, 1, keepdims=True), jnp.max(s_f, 1, keepdims=True))
        e_n = jnp.exp(s_n - top)
        e_f = jnp.exp(s_f - top)
        inv = 1.0 / (jnp.sum(e_n, 1, keepdims=True) + jnp.sum(e_f, 1, keepdims=True))
        p_n = e_n * inv
        p_f = e_f * inv
        delta = jnp.sum(p_n * dp_n, 1, keepdims=True) + jnp.sum(p_f * dp_f, 1, keepdims=True)
        ds_n = (p_n * (dp_n - delta)).astype(BF)
        ds_f = (p_f * (dp_f - delta)).astype(BF)
        p_n = p_n.astype(BF)
        p_f = p_f.astype(BF)
        gk_n = dot(ds_n, q, TN) * SCALE
        gv_n = dot(p_n, c, TN)
        gk_f = dot(ds_f, q, TN) * SCALE
        gv_f = dot(p_f, c, TN)
        for pack, g_n, g_f in ((head, gk_n, gk_f), (HEADS + head, gv_n, gv_f)):
            wide = slice(pack * HEAD_DIM, (pack + 1) * HEAD_DIM)
            edge_s[0, :, wide] = g_n[0:BLOCK].astype(BF)
            own_g[:, wide] = g_n[BLOCK:3 * BLOCK]
            edge_s[1, :, wide] = g_n[3 * BLOCK:].astype(BF)
            at = pack * COARSE
            for level in range(direct):
                part = g_f[level * COARSE:(level + 1) * COARSE].astype(BF)
                rows = rows_of(level)
                if rows >= 16:
                    for m in range(1 << level):
                        dst = level * TILE + m * PACK * rows + pack * rows
                        gsend[dst:dst + rows, :] = part[m * rows:(m + 1) * rows]
                else:
                    gtile[level, at:at + COARSE, :] = part
            for e in range(extra):
                xg_ref[e, at:at + COARSE, :] = g_f[
                    (direct + e) * COARSE:(direct + e + 1) * COARSE]
        att_ref[:, lane] = (
            dot(p_n, vn[:, lane], NN) + dot(p_f, fv, NN)
        ).astype(BF)
        qg_ref[:, lane] = (
            (dot(ds_n, kn[:, lane], NN) + dot(ds_f, fk, NN)) * SCALE
        ).astype(BF)

    def edge(side):
        dev = me - 1 if side == 0 else me + 1
        return pltpu.make_async_remote_copy(
            src_ref=edge_s.at[side], dst_ref=edge_r.at[1 - side],
            send_sem=ed_ss.at[side], recv_sem=ed_rs.at[side],
            device_id=where_is(dev), device_id_type=MESH,
        )

    @pl.when(has_prev)
    def _():
        edge(0).start()

    @pl.when(has_next)
    def _():
        edge(1).start()

    for level in reversed(range(direct)):
        if rows_of(level) < 16:
            gsend[level * TILE:(level + 1) * TILE, :] = dot(
                regroup(level, True), gtile[level], NN).astype(BF)
        size = PACK * rows_of(level)
        spread_out(
            level,
            lambda m, at=level * TILE, n=size: gsend.at[pl.ds(pl.multiple_of(at + m * n, n), n), :],
            grecv, dn_ss, dn_rs,
        )

    low_p, size_p = level_row_maps(direct, (TOK, 128), 1)
    pos_p = iota((TOK, 128), 0)
    share = jnp.where(
        (pos_p >= low_p) & (pos_p < low_p + size_p) & (pos_p < count), 1.0, 0.0
    ).astype(BF)
    share = jnp.concatenate([share, share], axis=1)

    gsum[:, row_offset(direct):, :] = jnp.zeros((PACK, 128 - row_offset(direct), 128), F32)
    for level in range(direct):
        whole = grecv.at[level * TILE:(level + 1) * TILE, :]
        pltpu.make_async_copy(whole, whole, dn_rs.at[level]).wait()
        rows = rows_of(level)
        n = PACK * rows
        total = grecv[level * TILE:level * TILE + n, :].astype(F32)
        for m in range(1, 1 << level):
            total = total + grecv[level * TILE + m * n:level * TILE + (m + 1) * n, :].astype(F32)
        at = row_offset(level)
        if rows >= 8:
            for pack in range(PACK):
                gsum[pack, at:at + rows, :] = total[pack * rows:(pack + 1) * rows]
        else:
            small[0:n, :] = total
            for pack in range(PACK):
                gsum[pack, at:at + rows, :] = small[pack * rows:(pack + 1) * rows, :]

    @pl.when(has_next)
    def _():
        edge(0).wait_recv()

    @pl.when(has_prev)
    def _():
        edge(1).wait_recv()

    for pack in range(PACK):
        wide = slice(pack * HEAD_DIM, (pack + 1) * HEAD_DIM)
        lane = slice((pack % HEADS) * HEAD_DIM, (pack % HEADS + 1) * HEAD_DIM)
        g = gsum[pack] / row_div
        high = g.astype(BF)
        rest_g = (g - high.astype(F32)).astype(BF)
        total = own_g[:, wide] + dot(share, jnp.concatenate([high, rest_g], axis=0), NN)
        total = total + jnp.concatenate([edge_r[0, :, wide], edge_r[1, :, wide]], 0).astype(F32)
        out = kg_ref if pack < HEADS else vg_ref
        out[:, lane] = total.astype(out.dtype)

    @pl.when(has_prev)
    def _():
        halo(0, 0).wait_send()
        halo(1, 0).wait_send()
        edge(0).wait_send()

    @pl.when(has_next)
    def _():
        halo(0, 1).wait_send()
        halo(1, 1).wait_send()
        edge(1).wait_send()

    for level in range(direct):
        whole = far.at[level * TILE:(level + 1) * TILE, :]
        pltpu.make_async_copy(whole, whole, up_ss.at[level]).wait()
        whole = grecv.at[level * TILE:(level + 1) * TILE, :]
        pltpu.make_async_copy(whole, whole, dn_ss.at[level]).wait()


def swapped(block, axis, stride):
    count = lax.axis_size(axis)
    route = [(i, i ^ (1 << stride)) for i in range(count)]
    return lax.ppermute(block, axis, route)


def halved(lower, upper):
    both = jnp.concatenate([lower, upper], axis=0)
    return both.reshape((both.shape[0] // 2, 2) + both.shape[1:]).sum(axis=1)


def ordered(side, own, other):
    return jnp.where(side == 0, own, other), jnp.where(side == 0, other, own)


def level_axes():
    shard_bits = lax.axis_size("shard").bit_length() - 1
    grp_bits = lax.axis_size("grp").bit_length() - 1
    return [("shard", i) for i in range(shard_bits)] + [("grp", i) for i in range(grp_bits)]


def climb(key_states, value_states, valid_mask, axes, direct):
    mask = valid_mask.astype(F32)
    kv = jnp.concatenate([key_states, value_states], axis=1).astype(F32)
    tile = (kv * mask[:, None]).reshape(COARSE, -1, 2 * WIDTH).sum(axis=1)
    count = mask.reshape(COARSE, -1).sum(axis=1)
    tiles = []
    counts = []
    for level, (axis, bit) in enumerate(axes):
        side = lax.axis_index(axis) >> bit & 1
        other, other_count = swapped((tile, count), axis, bit)
        if level >= direct:
            mean = (other / jnp.maximum(other_count, 1.0)[:, None]).astype(BF)
            marked = jnp.where(other_count[:, None] > 0, mean[:, :WIDTH], jnp.asarray(DEAD, BF))
            mean = jnp.concatenate([marked, mean[:, WIDTH:]], axis=1)
            tiles.append(
                mean.reshape(COARSE, PACK, HEAD_DIM).transpose(1, 0, 2).reshape(TILE, HEAD_DIM))
            counts.append(other_count)
        tile = halved(*ordered(side, tile, other))
        count = halved(*ordered(side, count, other_count))
    return jnp.stack(tiles), jnp.stack(counts)


def descend(grads, counts, axes, direct):
    zero = jnp.zeros((COARSE, 2 * WIDTH), F32)
    own = zero
    for level in reversed(range(len(axes))):
        axis, bit = axes[level]
        side = lax.axis_index(axis) >> bit & 1
        wide = jnp.repeat(own, 2, axis=0)
        mine, theirs = ordered(side, wide[:COARSE], wide[COARSE:])
        if level >= direct:
            part = grads[level - direct].reshape(PACK, COARSE, HEAD_DIM).transpose(1, 0, 2)
            part = part.reshape(COARSE, 2 * WIDTH)
            theirs = theirs + part / jnp.maximum(counts[level - direct], 1.0)[:, None]
        own = mine + swapped(theirs, axis, bit)
    return own


def body(query_states, key_states, value_states, valid_mask, attended_grad):
    axes = level_axes()
    n_grp = lax.axis_size("grp")
    n_shard = lax.axis_size("shard")
    direct = min(DIRECT, len(axes))
    extra = len(axes) - direct
    operands = [
        query_states, key_states, value_states, valid_mask.reshape(1, TOK), attended_grad]
    grad_type = F32 if extra else BF
    outs = [jax.ShapeDtypeStruct((TOK, WIDTH), t) for t in (BF, BF, grad_type, grad_type)]
    if extra:
        tiles, counts = climb(key_states, value_states, valid_mask, axes, direct)
        operands.append(tiles)
        outs.append(jax.ShapeDtypeStruct((extra, TILE, HEAD_DIM), F32))
    vmem = pl.BlockSpec(memory_space=pltpu.VMEM)
    dma = pltpu.SemaphoreType.DMA
    results = pl.pallas_call(
        functools.partial(kernel, n_grp, n_shard, direct, extra),
        out_shape=outs,
        in_specs=[vmem] * len(operands),
        out_specs=[vmem] * len(outs),
        scratch_shapes=[
            pltpu.VMEM((4 * BLOCK, WIDTH), BF),
            pltpu.VMEM((4 * BLOCK, WIDTH), BF),
            pltpu.VMEM((up_offset(direct), HEAD_DIM), BF),
            pltpu.VMEM((direct * TILE, HEAD_DIM), BF),
            pltpu.VMEM((direct + extra, TILE, HEAD_DIM), BF),
            pltpu.VMEM((128, HEAD_DIM), F32),
            pltpu.VMEM((HEADS, TOK, 4 * BLOCK), F32),
            pltpu.VMEM((HEADS, TOK, 4 * BLOCK), F32),
            pltpu.VMEM((TOK, 2 * WIDTH), F32),
            pltpu.VMEM((2, BLOCK, 2 * WIDTH), BF),
            pltpu.VMEM((2, BLOCK, 2 * WIDTH), BF),
            pltpu.VMEM((direct, TILE, HEAD_DIM), BF),
            pltpu.VMEM((direct * TILE, HEAD_DIM), BF),
            pltpu.VMEM((direct * TILE, HEAD_DIM), BF),
            pltpu.VMEM((PACK, 128, HEAD_DIM), F32),
            dma((4,)),
            dma((4,)),
            dma((direct,)),
            dma((direct,)),
            dma((2,)),
            dma((2,)),
            dma((direct,)),
            dma((direct,)),
        ],
        compiler_params=pltpu.CompilerParams(
            collective_id=0, has_side_effects=True, vmem_limit_bytes=48 * 1024 * 1024
        ),
    )(*operands)
    if not extra:
        return tuple(results)
    attended, query_grad, key_grad, value_grad, grads = results
    own = descend(grads, counts, axes, direct)
    spread = jnp.repeat(own, TOK // COARSE, axis=0) * valid_mask.astype(F32)[:, None]
    return (
        attended,
        query_grad,
        (key_grad + spread[:, :WIDTH]).astype(BF),
        (value_grad + spread[:, WIDTH:]).astype(BF),
    )


def solution(mesh):
    rows = P(("grp", "shard"), None)
    return jax.shard_map(
        body,
        mesh=mesh,
        in_specs=(rows, rows, rows, P(("grp", "shard")), rows),
        out_specs=(rows, rows, rows, rows),
        check_vma=False,
    )
```

```python
import functools

import jax
import jax.numpy as jnp
from jax import lax
from jax.experimental import pallas as pl
from jax.experimental.pallas import tpu as pltpu
from jax.sharding import PartitionSpec as P

HEADS = 4
HEAD_DIM = 128
BLOCK = 128
COARSE = 64
DIRECT = 5
TOK = 256
WIDTH = HEADS * HEAD_DIM
PACK = 2 * HEADS
TILE = PACK * COARSE
SCALE = HEAD_DIM ** (-0.5)
MASKED = -1e30
DEAD = 1024.0
DEAD_SUM = 65536.0
MESH = pl.DeviceIdType.MESH
BF = jnp.bfloat16
F32 = jnp.float32


def rows_of(level):
    return COARSE >> level


def up_offset(level):
    return sum(PACK * rows_of(i) for i in range(level))


def row_offset(level):
    return sum(rows_of(i) for i in range(level))


def iota(shape, dim):
    return lax.broadcasted_iota(jnp.int32, shape, dim)


def dot(a, b, dims):
    return lax.dot_general(a, b, (dims, ((), ())), preferred_element_type=F32)


NN = ((1,), (0,))
NT = ((1,), (1,))
TN = ((0,), (0,))


CHUNK = 64
NEAR = 4 * BLOCK


def level_row_maps(direct, shape, dim):
    idx = iota(shape, dim)
    low = jnp.full(shape, 2 * TOK, jnp.int32)
    size = jnp.ones(shape, jnp.int32)
    for level in range(direct):
        group = 4 << level
        at = row_offset(level)
        inside = (idx >= at) & (idx < at + rows_of(level))
        low = jnp.where(inside, (idx - at) * group, low)
        size = jnp.where(inside, group, size)
    return low, size


def kernel(
    n_grp, n_shard, direct, extra,
    q_in, k_in, v_in, m_ref, c_in, *rest,
):
    if extra:
        xt_ref, att_ref, qg_ref, kg_ref, vg_ref, xg_ref, *rest = rest
    else:
        att_ref, qg_ref, kg_ref, vg_ref, *rest = rest
    (q_ref, k_ref, v_ref, c_ref, in_sem, kn, vn, up, far, ftile, small, mixed, mixed2, bias, score, dp,
     p_t, ds_t, own_g, edge_s, edge_r, gsend, grecv, gsum,
     halo_ss, halo_rs, up_ss, up_rs, ed_ss, ed_rs, dn_ss, dn_rs) = rest
    loads = [
        pltpu.make_async_copy(src, dst, in_sem.at[i])
        for i, (src, dst) in enumerate(
            ((k_in, k_ref), (v_in, v_ref), (q_in, q_ref), (c_in, c_ref)))
    ]
    for load in loads:
        load.start()
    n_dev = n_grp * n_shard
    me = lax.axis_index("grp") * n_shard + lax.axis_index("shard")
    span = 1 << direct
    far_rows = (direct + extra) * COARSE

    def where_is(dev):
        return (dev // n_shard, dev % n_shard)

    def sibling(level):
        part = me // (1 << level)
        return (part + 1 - 2 * (part % 2)) * (1 << level)

    base = (me // span) * span
    at_low = me == base
    at_high = me == base + span - 1
    has_prev = me > 0
    has_next = me < n_dev - 1
    out_prev = has_prev & at_low
    out_next = has_next & at_high
    barrier = pltpu.get_barrier_semaphore()

    def hello(t, _):
        pl.semaphore_signal(
            barrier, inc=1, device_id=where_is(base + (me - base + t) % span), device_id_type=MESH
        )
        return 0

    lax.fori_loop(1, span, hello, 0)
    if n_dev > span:
        @pl.when(out_prev)
        def _():
            pl.semaphore_signal(barrier, inc=1, device_id=where_is(me - 1), device_id_type=MESH)

        @pl.when(out_next)
        def _():
            pl.semaphore_signal(barrier, inc=1, device_id=where_is(me + 1), device_id_type=MESH)

    loads[0].wait()
    loads[1].wait()

    count = jnp.sum(m_ref[...], axis=1, keepdims=True)
    live_col = iota((TOK, 1), 0) < count
    kn[BLOCK:BLOCK + TOK, :] = jnp.where(live_col, k_ref[...].astype(F32), DEAD).astype(BF)
    vn[BLOCK:BLOCK + TOK, :] = v_ref[...]
    low, size = level_row_maps(direct, (128, TOK), 0)
    pos = iota((128, TOK), 1)
    pool = jnp.where((pos >= low) & (pos < low + size) & (pos < count), 1.0, 0.0).astype(BF)
    low_c, size_c = level_row_maps(direct, (128, 1), 0)
    row_count = jnp.clip(count - low_c, 0, size_c).astype(F32)
    row_div = jnp.maximum(row_count, 1.0)
    for pack in range(PACK):
        ref = k_ref if pack < HEADS else v_ref
        lane = (pack % HEADS) * HEAD_DIM
        mean = dot(pool, ref[:, lane:lane + HEAD_DIM], NN) / row_div
        if pack < HEADS:
            mean = jnp.where(row_count > 0, mean, DEAD)
        for level in range(direct):
            rows = rows_of(level)
            part = mean[row_offset(level):row_offset(level) + rows]
            if rows >= 16:
                at = up_offset(level) + pack * rows
                up[at:at + rows, :] = part.astype(BF)
            else:
                at = up_offset(level) - up_offset(3) + pack * rows
                small[at:at + rows, :] = part
    if direct > 3:
        tail = up_offset(direct) - up_offset(3)
        up[up_offset(3):up_offset(direct), :] = small[0:tail, :].astype(BF)

    pl.semaphore_wait(barrier, span - 1)
    if n_dev > span:
        @pl.when(out_prev)
        def _():
            pl.semaphore_wait(barrier, 1)

        @pl.when(out_next)
        def _():
            pl.semaphore_wait(barrier, 1)

    def halo(which, side):
        ref = kn if which == 0 else vn
        slot = 2 * which + side
        if side == 0:
            src, dst, dev = ref.at[BLOCK:2 * BLOCK, :], ref.at[3 * BLOCK:4 * BLOCK, :], me - 1
        else:
            src, dst, dev = ref.at[2 * BLOCK:3 * BLOCK, :], ref.at[0:BLOCK, :], me + 1
        return pltpu.make_async_remote_copy(
            src_ref=src, dst_ref=dst, send_sem=halo_ss.at[slot], recv_sem=halo_rs.at[slot],
            device_id=where_is(dev), device_id_type=MESH,
        )

    @pl.when(has_prev)
    def _():
        halo(0, 0).start()
        halo(1, 0).start()

    @pl.when(has_next)
    def _():
        halo(0, 1).start()
        halo(1, 1).start()

    @pl.when(jnp.logical_not(has_prev))
    def _():
        kn[0:BLOCK, :] = jnp.full((BLOCK, WIDTH), DEAD, BF)
        vn[0:BLOCK, :] = jnp.zeros((BLOCK, WIDTH), BF)
        edge_r[0] = jnp.zeros((BLOCK, 2 * WIDTH), BF)

    @pl.when(jnp.logical_not(has_next))
    def _():
        kn[3 * BLOCK:4 * BLOCK, :] = jnp.full((BLOCK, WIDTH), DEAD, BF)
        vn[3 * BLOCK:4 * BLOCK, :] = jnp.zeros((BLOCK, WIDTH), BF)
        edge_r[1] = jnp.zeros((BLOCK, 2 * WIDTH), BF)

    def spread_out(level, source, target, send_sem, recv_sem):
        size = PACK * rows_of(level)
        parts = 1 << level
        to = sibling(level)
        land = pl.multiple_of(level * TILE + (me % parts) * size, size)

        def send(t, _):
            m = (me + t) % parts
            pltpu.make_async_remote_copy(
                src_ref=source(m), dst_ref=target.at[pl.ds(land, size), :],
                send_sem=send_sem.at[level], recv_sem=recv_sem.at[level],
                device_id=where_is(to + m), device_id_type=MESH,
            ).start()
            return 0

        if parts == 1:
            send(0, 0)
        else:
            lax.fori_loop(0, parts, send, 0)

    for level in reversed(range(direct)):
        at = up_offset(level)
        spread_out(
            level, lambda m, at=at, n=PACK * rows_of(level): up.at[at:at + n, :], far, up_ss, up_rs
        )

    @pl.when(has_next)
    def _():
        halo(0, 0).wait_recv()
        halo(1, 0).wait_recv()

    @pl.when(has_prev)
    def _():
        halo(0, 1).wait_recv()
        halo(1, 1).wait_recv()

    loads[2].wait()
    loads[3].wait()
    block_col = iota((1, TOK), 1) // BLOCK
    for at in range(0, NEAR, CHUNK):
        mark = jnp.where(kn[at:at + CHUNK, 0:HEAD_DIM].astype(F32)[:, 0:1] > DEAD / 2, MASKED, 0.0)
        mark = jnp.broadcast_to(mark, (CHUNK, TOK))
        if at < BLOCK:
            mark = jnp.where(block_col == 0, mark, MASKED)
        if at >= 3 * BLOCK:
            mark = jnp.where(block_col == 1, mark, MASKED)
        bias[at:at + CHUNK, :] = mark
    for head in range(HEADS):
        lane = slice(head * HEAD_DIM, (head + 1) * HEAD_DIM)
        score[head, 0:NEAR, :] = dot(kn[:, lane], q_ref[:, lane], NT)
        dp[head, 0:NEAR, :] = dot(vn[:, lane], c_ref[:, lane], NT)

    for level in range(direct):
        whole = far.at[level * TILE:(level + 1) * TILE, :]
        pltpu.make_async_copy(whole, whole, up_rs.at[level]).wait()
        rows = rows_of(level)
        at = level * COARSE
        if rows >= 16:
            for m in range(1 << level):
                for pack in range(PACK):
                    src = level * TILE + (m * PACK + pack) * rows
                    ftile[pack, at + m * rows:at + (m + 1) * rows, :] = far[src:src + rows, :]
        else:
            mixed[...] = whole[...].astype(F32)
            for pack in range(PACK):
                for m in range(1 << level):
                    src = (m * PACK + pack) * rows
                    small[m * rows:(m + 1) * rows, :] = mixed[src:src + rows, :]
                ftile[pack, at:at + COARSE, :] = small[0:COARSE, :].astype(BF)
    for e in range(extra):
        at = (direct + e) * COARSE
        for pack in range(PACK):
            ftile[pack, at:at + COARSE, :] = xt_ref[e, pack * COARSE:(pack + 1) * COARSE, :]
    for at in range(0, far_rows, CHUNK):
        mark = jnp.where(ftile[0, at:at + CHUNK, :].astype(F32)[:, 0:1] > DEAD / 2, MASKED, 0.0)
        bias[NEAR + at:NEAR + at + CHUNK, :] = jnp.broadcast_to(mark, (CHUNK, TOK))

    def fold(value, op):
        return op(value.reshape(CHUNK // 8, 8, TOK), 0)

    for head in range(HEADS):
        lane = slice(head * HEAD_DIM, (head + 1) * HEAD_DIM)
        q = q_ref[:, lane]
        c = c_ref[:, lane]
        fk = ftile.at[head]
        fv = ftile.at[HEADS + head]
        score[head, NEAR:, :] = dot(fk[...], q, NT)
        dp[head, NEAR:, :] = dot(fv[...], c, NT)
        top = jnp.full((8, TOK), MASKED, F32)
        for at in range(0, NEAR + far_rows, CHUNK):
            t = score[head, at:at + CHUNK, :] * SCALE + bias[at:at + CHUNK, :]
            score[head, at:at + CHUNK, :] = t
            top = jnp.maximum(top, fold(t, jnp.max))
        top = jnp.max(top, 0, keepdims=True)
        z = jnp.zeros((8, TOK), F32)
        d = jnp.zeros((8, TOK), F32)
        for at in range(0, NEAR + far_rows, CHUNK):
            e = jnp.exp(score[head, at:at + CHUNK, :] - top)
            score[head, at:at + CHUNK, :] = e
            z = z + fold(e, jnp.sum)
            d = d + fold(e * dp[head, at:at + CHUNK, :], jnp.sum)
        inv = 1.0 / jnp.sum(z, 0, keepdims=True)
        delta = jnp.sum(d, 0, keepdims=True) * inv
        for at in range(0, NEAR + far_rows, CHUNK):
            p = score[head, at:at + CHUNK, :] * inv
            p_t[at:at + CHUNK, :] = p.astype(BF)
            ds_t[at:at + CHUNK, :] = (p * (dp[head, at:at + CHUNK, :] - delta)).astype(BF)
        gk = dot(ds_t[...], q, NN) * SCALE
        gv = dot(p_t[...], c, NN)
        for pack, g in ((head, gk), (HEADS + head, gv)):
            wide = slice(pack * HEAD_DIM, (pack + 1) * HEAD_DIM)
            edge_s[0, :, wide] = g[0:BLOCK].astype(BF)
            own_g[:, wide] = g[BLOCK:3 * BLOCK]
            edge_s[1, :, wide] = g[3 * BLOCK:NEAR].astype(BF)
            for level in range(direct):
                at = NEAR + level * COARSE
                rows = rows_of(level)
                part = g[at:at + COARSE]
                if rows >= 16:
                    for m in range(1 << level):
                        dst = level * TILE + (m * PACK + pack) * rows
                        gsend[dst:dst + rows, :] = part[m * rows:(m + 1) * rows].astype(BF)
                else:
                    small[0:COARSE, :] = part
                    for m in range(1 << level):
                        dst = (m * PACK + pack) * rows
                        mixed_g = mixed if level == 3 else mixed2
                        mixed_g[dst:dst + rows, :] = small[m * rows:(m + 1) * rows, :]
            for e in range(extra):
                at = NEAR + (direct + e) * COARSE
                xg_ref[e, pack * COARSE:(pack + 1) * COARSE, :] = g[at:at + COARSE]
        out = dot(vn[:, lane], p_t[0:NEAR, :], TN) + dot(fv[...], p_t[NEAR:, :], TN)
        att_ref[:, lane] = out.T.astype(BF)
        out = dot(kn[:, lane], ds_t[0:NEAR, :], TN) + dot(fk[...], ds_t[NEAR:, :], TN)
        qg_ref[:, lane] = (out * SCALE).T.astype(BF)

    def edge(side):
        dev = me - 1 if side == 0 else me + 1
        return pltpu.make_async_remote_copy(
            src_ref=edge_s.at[side], dst_ref=edge_r.at[1 - side],
            send_sem=ed_ss.at[side], recv_sem=ed_rs.at[side],
            device_id=where_is(dev), device_id_type=MESH,
        )

    @pl.when(has_prev)
    def _():
        edge(0).start()

    @pl.when(has_next)
    def _():
        edge(1).start()

    for level in reversed(range(direct)):
        if rows_of(level) < 16:
            regrouped = mixed if level == 3 else mixed2
            gsend[level * TILE:(level + 1) * TILE, :] = regrouped[...].astype(BF)
        size = PACK * rows_of(level)
        spread_out(
            level,
            lambda m, at=level * TILE, n=size: gsend.at[pl.ds(pl.multiple_of(at + m * n, n), n), :],
            grecv, dn_ss, dn_rs,
        )

    low_p, size_p = level_row_maps(direct, (TOK, 128), 1)
    pos_p = iota((TOK, 128), 0)
    share = jnp.where(
        (pos_p >= low_p) & (pos_p < low_p + size_p) & (pos_p < count), 1.0, 0.0
    ).astype(BF)
    share = jnp.concatenate([share, share], axis=1)

    gsum[:, row_offset(direct):, :] = jnp.zeros((PACK, 128 - row_offset(direct), 128), F32)
    for level in range(direct):
        whole = grecv.at[level * TILE:(level + 1) * TILE, :]
        pltpu.make_async_copy(whole, whole, dn_rs.at[level]).wait()
        rows = rows_of(level)
        n = PACK * rows
        total = grecv[level * TILE:level * TILE + n, :].astype(F32)
        for m in range(1, 1 << level):
            total = total + grecv[level * TILE + m * n:level * TILE + (m + 1) * n, :].astype(F32)
        at = row_offset(level)
        if rows >= 8:
            for pack in range(PACK):
                gsum[pack, at:at + rows, :] = total[pack * rows:(pack + 1) * rows]
        else:
            small[0:n, :] = total
            for pack in range(PACK):
                gsum[pack, at:at + rows, :] = small[pack * rows:(pack + 1) * rows, :]

    @pl.when(has_next)
    def _():
        edge(0).wait_recv()

    @pl.when(has_prev)
    def _():
        edge(1).wait_recv()

    for pack in range(PACK):
        wide = slice(pack * HEAD_DIM, (pack + 1) * HEAD_DIM)
        lane = slice((pack % HEADS) * HEAD_DIM, (pack % HEADS + 1) * HEAD_DIM)
        g = gsum[pack] / row_div
        high = g.astype(BF)
        rest_g = (g - high.astype(F32)).astype(BF)
        total = own_g[:, wide] + dot(share, jnp.concatenate([high, rest_g], axis=0), NN)
        total = total + jnp.concatenate([edge_r[0, :, wide], edge_r[1, :, wide]], 0).astype(F32)
        out = kg_ref if pack < HEADS else vg_ref
        out[:, lane] = total.astype(out.dtype)

    @pl.when(has_prev)
    def _():
        halo(0, 0).wait_send()
        halo(1, 0).wait_send()
        edge(0).wait_send()

    @pl.when(has_next)
    def _():
        halo(0, 1).wait_send()
        halo(1, 1).wait_send()
        edge(1).wait_send()

    for level in range(direct):
        whole = far.at[level * TILE:(level + 1) * TILE, :]
        pltpu.make_async_copy(whole, whole, up_ss.at[level]).wait()
        whole = grecv.at[level * TILE:(level + 1) * TILE, :]
        pltpu.make_async_copy(whole, whole, dn_ss.at[level]).wait()


def swapped(block, axis, stride):
    count = lax.axis_size(axis)
    route = [(i, i ^ (1 << stride)) for i in range(count)]
    return lax.ppermute(block, axis, route)


def halved(lower, upper):
    both = jnp.concatenate([lower, upper], axis=0)
    return both.reshape((both.shape[0] // 2, 2) + both.shape[1:]).sum(axis=1)


def ordered(side, own, other):
    return jnp.where(side == 0, own, other), jnp.where(side == 0, other, own)


def level_axes():
    shard_bits = lax.axis_size("shard").bit_length() - 1
    grp_bits = lax.axis_size("grp").bit_length() - 1
    return [("shard", i) for i in range(shard_bits)] + [("grp", i) for i in range(grp_bits)]


def climb(key_states, value_states, valid_mask, axes, direct):
    mask = valid_mask.astype(F32)
    kv = jnp.concatenate([key_states, value_states], axis=1).astype(F32)
    tile = (kv * mask[:, None]).reshape(COARSE, -1, 2 * WIDTH).sum(axis=1)
    count = mask.reshape(COARSE, -1).sum(axis=1)
    tiles = []
    counts = []
    for level, (axis, bit) in enumerate(axes):
        side = lax.axis_index(axis) >> bit & 1
        other, other_count = swapped((tile, count), axis, bit)
        if level >= direct:
            mean = (other / jnp.maximum(other_count, 1.0)[:, None]).astype(BF)
            marked = jnp.where(other_count[:, None] > 0, mean[:, :WIDTH], jnp.asarray(DEAD, BF))
            mean = jnp.concatenate([marked, mean[:, WIDTH:]], axis=1)
            tiles.append(
                mean.reshape(COARSE, PACK, HEAD_DIM).transpose(1, 0, 2).reshape(TILE, HEAD_DIM))
            counts.append(other_count)
        tile = halved(*ordered(side, tile, other))
        count = halved(*ordered(side, count, other_count))
    return jnp.stack(tiles), jnp.stack(counts)


def descend(grads, counts, axes, direct):
    zero = jnp.zeros((COARSE, 2 * WIDTH), F32)
    own = zero
    for level in reversed(range(len(axes))):
        axis, bit = axes[level]
        side = lax.axis_index(axis) >> bit & 1
        wide = jnp.repeat(own, 2, axis=0)
        mine, theirs = ordered(side, wide[:COARSE], wide[COARSE:])
        if level >= direct:
            part = grads[level - direct].reshape(PACK, COARSE, HEAD_DIM).transpose(1, 0, 2)
            part = part.reshape(COARSE, 2 * WIDTH)
            theirs = theirs + part / jnp.maximum(counts[level - direct], 1.0)[:, None]
        own = mine + swapped(theirs, axis, bit)
    return own


def body(query_states, key_states, value_states, valid_mask, attended_grad):
    axes = level_axes()
    n_grp = lax.axis_size("grp")
    n_shard = lax.axis_size("shard")
    direct = min(DIRECT, len(axes))
    extra = len(axes) - direct
    operands = [
        query_states, key_states, value_states, valid_mask.reshape(1, TOK), attended_grad]
    grad_type = F32 if extra else BF
    outs = [jax.ShapeDtypeStruct((TOK, WIDTH), t) for t in (BF, BF, grad_type, grad_type)]
    if extra:
        tiles, counts = climb(key_states, value_states, valid_mask, axes, direct)
        operands.append(tiles)
        outs.append(jax.ShapeDtypeStruct((extra, TILE, HEAD_DIM), F32))
    vmem = pl.BlockSpec(memory_space=pltpu.VMEM)
    anywhere = pl.BlockSpec(memory_space=pl.ANY)
    dma = pltpu.SemaphoreType.DMA
    all_rows = NEAR + (direct + extra) * COARSE
    results = pl.pallas_call(
        functools.partial(kernel, n_grp, n_shard, direct, extra),
        out_shape=outs,
        in_specs=[anywhere] * 3 + [vmem, anywhere] + [vmem] * (len(operands) - 5),
        out_specs=[vmem] * len(outs),
        scratch_shapes=[
            pltpu.VMEM((TOK, WIDTH), BF),
            pltpu.VMEM((TOK, WIDTH), BF),
            pltpu.VMEM((TOK, WIDTH), BF),
            pltpu.VMEM((TOK, WIDTH), BF),
            dma((4,)),
            pltpu.VMEM((NEAR, WIDTH), BF),
            pltpu.VMEM((NEAR, WIDTH), BF),
            pltpu.VMEM((up_offset(direct), HEAD_DIM), BF),
            pltpu.VMEM((direct * TILE, HEAD_DIM), BF),
            pltpu.VMEM((PACK, (direct + extra) * COARSE, HEAD_DIM), BF),
            pltpu.VMEM((128, HEAD_DIM), F32),
            pltpu.VMEM((TILE, HEAD_DIM), F32),
            pltpu.VMEM((TILE, HEAD_DIM), F32),
            pltpu.VMEM((all_rows, TOK), F32),
            pltpu.VMEM((HEADS, all_rows, TOK), F32),
            pltpu.VMEM((HEADS, all_rows, TOK), F32),
            pltpu.VMEM((all_rows, TOK), BF),
            pltpu.VMEM((all_rows, TOK), BF),
            pltpu.VMEM((TOK, 2 * WIDTH), F32),
            pltpu.VMEM((2, BLOCK, 2 * WIDTH), BF),
            pltpu.VMEM((2, BLOCK, 2 * WIDTH), BF),
            pltpu.VMEM((direct * TILE, HEAD_DIM), BF),
            pltpu.VMEM((direct * TILE, HEAD_DIM), BF),
            pltpu.VMEM((PACK, 128, HEAD_DIM), F32),
            dma((4,)),
            dma((4,)),
            dma((direct,)),
            dma((direct,)),
            dma((2,)),
            dma((2,)),
            dma((direct,)),
            dma((direct,)),
        ],
        compiler_params=pltpu.CompilerParams(
            collective_id=0, has_side_effects=True, vmem_limit_bytes=48 * 1024 * 1024
        ),
    )(*operands)
    if not extra:
        return tuple(results)
    attended, query_grad, key_grad, value_grad, grads = results
    own = descend(grads, counts, axes, direct)
    spread = jnp.repeat(own, TOK // COARSE, axis=0) * valid_mask.astype(F32)[:, None]
    return (
        attended,
        query_grad,
        (key_grad + spread[:, :WIDTH]).astype(BF),
        (value_grad + spread[:, WIDTH:]).astype(BF),
    )


def solution(mesh):
    rows = P(("grp", "shard"), None)
    return jax.shard_map(
        body,
        mesh=mesh,
        in_specs=(rows, rows, rows, P(("grp", "shard")), rows),
        out_specs=(rows, rows, rows, rows),
        check_vma=False,
    )
```

```python
import functools

import jax
import jax.numpy as jnp
from jax import lax
from jax.experimental import pallas as pl
from jax.experimental.pallas import tpu as pltpu
from jax.sharding import PartitionSpec as P

HEADS = 4
HEAD_DIM = 128
BLOCK = 128
COARSE = 64
DIRECT = 5
TOK = 256
WIDTH = HEADS * HEAD_DIM
PACK = 2 * HEADS
TILE = PACK * COARSE
SCALE = HEAD_DIM ** (-0.5)
MASKED = -1e30
DEAD = 1024.0
DEAD_SUM = 65536.0
MESH = pl.DeviceIdType.MESH
BF = jnp.bfloat16
F32 = jnp.float32


def rows_of(level):
    return COARSE >> level


def up_offset(level):
    return sum(PACK * rows_of(i) for i in range(level))


def row_offset(level):
    return sum(rows_of(i) for i in range(level))


def iota(shape, dim):
    return lax.broadcasted_iota(jnp.int32, shape, dim)


def dot(a, b, dims):
    return lax.dot_general(a, b, (dims, ((), ())), preferred_element_type=F32)


NN = ((1,), (0,))
NT = ((1,), (1,))
TN = ((0,), (0,))


CHUNK = 64
NEAR = 4 * BLOCK


def level_row_maps(direct, shape, dim):
    idx = iota(shape, dim)
    low = jnp.full(shape, 2 * TOK, jnp.int32)
    size = jnp.ones(shape, jnp.int32)
    for level in range(direct):
        group = 4 << level
        at = row_offset(level)
        inside = (idx >= at) & (idx < at + rows_of(level))
        low = jnp.where(inside, (idx - at) * group, low)
        size = jnp.where(inside, group, size)
    return low, size


def kernel(
    n_grp, n_shard, direct, extra,
    q_in, k_in, v_in, m_in, c_in, *rest,
):
    if extra:
        xt_ref, *outs_hbm, xg_ref = rest[:6]
        rest = rest[6:]
    else:
        outs_hbm = rest[:4]
        rest = rest[4:]
    (att_ref, qg_ref, kg_ref, vg_ref, out_sem, q_ref, k_ref, v_ref, c_ref, m_ref, in_sem, kn, vn, up, far, ftile, small, mixed, mixed2, bias, score, dp,
     p_t, ds_t, own_g, edge_s, edge_r, gsend, grecv, gsum,
     halo_ss, halo_rs, up_ss, up_rs, ed_ss, ed_rs, dn_ss, dn_rs) = rest
    loads = [
        pltpu.make_async_copy(src, dst, in_sem.at[i])
        for i, (src, dst) in enumerate(
            ((k_in, k_ref), (v_in, v_ref), (q_in, q_ref), (c_in, c_ref), (m_in, m_ref)))
    ]
    for load in loads:
        load.start()
    stores = [
        pltpu.make_async_copy(src, dst, out_sem.at[i])
        for i, (src, dst) in enumerate(zip((att_ref, qg_ref, kg_ref, vg_ref), outs_hbm))
    ]
    n_dev = n_grp * n_shard
    me = lax.axis_index("grp") * n_shard + lax.axis_index("shard")
    span = 1 << direct
    far_rows = (direct + extra) * COARSE

    def where_is(dev):
        return (dev // n_shard, dev % n_shard)

    def sibling(level):
        part = me // (1 << level)
        return (part + 1 - 2 * (part % 2)) * (1 << level)

    base = (me // span) * span
    at_low = me == base
    at_high = me == base + span - 1
    has_prev = me > 0
    has_next = me < n_dev - 1
    out_prev = has_prev & at_low
    out_next = has_next & at_high
    barrier = pltpu.get_barrier_semaphore()

    def hello(t, _):
        pl.semaphore_signal(
            barrier, inc=1, device_id=where_is(base + (me - base + t) % span), device_id_type=MESH
        )
        return 0

    lax.fori_loop(1, span, hello, 0)
    if n_dev > span:
        @pl.when(out_prev)
        def _():
            pl.semaphore_signal(barrier, inc=1, device_id=where_is(me - 1), device_id_type=MESH)

        @pl.when(out_next)
        def _():
            pl.semaphore_signal(barrier, inc=1, device_id=where_is(me + 1), device_id_type=MESH)

    loads[0].wait()
    loads[1].wait()
    loads[4].wait()

    count = jnp.sum(m_ref[...], axis=1, keepdims=True)
    live_col = iota((TOK, 1), 0) < count
    kn[BLOCK:BLOCK + TOK, :] = jnp.where(live_col, k_ref[...].astype(F32), DEAD).astype(BF)
    vn[BLOCK:BLOCK + TOK, :] = v_ref[...]
    low, size = level_row_maps(direct, (128, TOK), 0)
    pos = iota((128, TOK), 1)
    pool = jnp.where((pos >= low) & (pos < low + size) & (pos < count), 1.0, 0.0).astype(BF)
    low_c, size_c = level_row_maps(direct, (128, 1), 0)
    row_count = jnp.clip(count - low_c, 0, size_c).astype(F32)
    row_div = jnp.maximum(row_count, 1.0)
    for pack in range(PACK):
        ref = k_ref if pack < HEADS else v_ref
        lane = (pack % HEADS) * HEAD_DIM
        mean = dot(pool, ref[:, lane:lane + HEAD_DIM], NN) / row_div
        if pack < HEADS:
            mean = jnp.where(row_count > 0, mean, DEAD)
        for level in range(direct):
            rows = rows_of(level)
            part = mean[row_offset(level):row_offset(level) + rows]
            if rows >= 16:
                at = up_offset(level) + pack * rows
                up[at:at + rows, :] = part.astype(BF)
            else:
                at = up_offset(level) - up_offset(3) + pack * rows
                small[at:at + rows, :] = part
    if direct > 3:
        tail = up_offset(direct) - up_offset(3)
        up[up_offset(3):up_offset(direct), :] = small[0:tail, :].astype(BF)

    pl.semaphore_wait(barrier, span - 1)
    if n_dev > span:
        @pl.when(out_prev)
        def _():
            pl.semaphore_wait(barrier, 1)

        @pl.when(out_next)
        def _():
            pl.semaphore_wait(barrier, 1)

    def halo(which, side):
        ref = kn if which == 0 else vn
        slot = 2 * which + side
        if side == 0:
            src, dst, dev = ref.at[BLOCK:2 * BLOCK, :], ref.at[3 * BLOCK:4 * BLOCK, :], me - 1
        else:
            src, dst, dev = ref.at[2 * BLOCK:3 * BLOCK, :], ref.at[0:BLOCK, :], me + 1
        return pltpu.make_async_remote_copy(
            src_ref=src, dst_ref=dst, send_sem=halo_ss.at[slot], recv_sem=halo_rs.at[slot],
            device_id=where_is(dev), device_id_type=MESH,
        )

    @pl.when(has_prev)
    def _():
        halo(0, 0).start()
        halo(1, 0).start()

    @pl.when(has_next)
    def _():
        halo(0, 1).start()
        halo(1, 1).start()

    @pl.when(jnp.logical_not(has_prev))
    def _():
        kn[0:BLOCK, :] = jnp.full((BLOCK, WIDTH), DEAD, BF)
        vn[0:BLOCK, :] = jnp.zeros((BLOCK, WIDTH), BF)
        edge_r[0] = jnp.zeros((BLOCK, 2 * WIDTH), BF)

    @pl.when(jnp.logical_not(has_next))
    def _():
        kn[3 * BLOCK:4 * BLOCK, :] = jnp.full((BLOCK, WIDTH), DEAD, BF)
        vn[3 * BLOCK:4 * BLOCK, :] = jnp.zeros((BLOCK, WIDTH), BF)
        edge_r[1] = jnp.zeros((BLOCK, 2 * WIDTH), BF)

    def spread_out(level, source, target, send_sem, recv_sem):
        size = PACK * rows_of(level)
        parts = 1 << level
        to = sibling(level)
        land = pl.multiple_of(level * TILE + (me % parts) * size, size)

        def send(t, _):
            m = (me + t) % parts
            pltpu.make_async_remote_copy(
                src_ref=source(m), dst_ref=target.at[pl.ds(land, size), :],
                send_sem=send_sem.at[level], recv_sem=recv_sem.at[level],
                device_id=where_is(to + m), device_id_type=MESH,
            ).start()
            return 0

        if parts == 1:
            send(0, 0)
        else:
            lax.fori_loop(0, parts, send, 0)

    for level in reversed(range(direct)):
        at = up_offset(level)
        spread_out(
            level, lambda m, at=at, n=PACK * rows_of(level): up.at[at:at + n, :], far, up_ss, up_rs
        )

    @pl.when(has_next)
    def _():
        halo(0, 0).wait_recv()
        halo(1, 0).wait_recv()

    @pl.when(has_prev)
    def _():
        halo(0, 1).wait_recv()
        halo(1, 1).wait_recv()

    loads[2].wait()
    loads[3].wait()
    block_col = iota((1, TOK), 1) // BLOCK
    for at in range(0, NEAR, CHUNK):
        mark = jnp.where(kn[at:at + CHUNK, 0:HEAD_DIM].astype(F32)[:, 0:1] > DEAD / 2, MASKED, 0.0)
        mark = jnp.broadcast_to(mark, (CHUNK, TOK))
        if at < BLOCK:
            mark = jnp.where(block_col == 0, mark, MASKED)
        if at >= 3 * BLOCK:
            mark = jnp.where(block_col == 1, mark, MASKED)
        bias[at:at + CHUNK, :] = mark
    for head in range(HEADS):
        lane = slice(head * HEAD_DIM, (head + 1) * HEAD_DIM)
        score[head, 0:NEAR, :] = dot(kn[:, lane], q_ref[:, lane], NT)
        dp[head, 0:NEAR, :] = dot(vn[:, lane], c_ref[:, lane], NT)

    for level in range(direct):
        whole = far.at[level * TILE:(level + 1) * TILE, :]
        pltpu.make_async_copy(whole, whole, up_rs.at[level]).wait()
        rows = rows_of(level)
        at = level * COARSE
        if rows >= 16:
            for m in range(1 << level):
                for pack in range(PACK):
                    src = level * TILE + (m * PACK + pack) * rows
                    ftile[pack, at + m * rows:at + (m + 1) * rows, :] = far[src:src + rows, :]
        else:
            mixed[...] = whole[...].astype(F32)
            for pack in range(PACK):
                for m in range(1 << level):
                    src = (m * PACK + pack) * rows
                    small[m * rows:(m + 1) * rows, :] = mixed[src:src + rows, :]
                ftile[pack, at:at + COARSE, :] = small[0:COARSE, :].astype(BF)
    for e in range(extra):
        at = (direct + e) * COARSE
        for pack in range(PACK):
            ftile[pack, at:at + COARSE, :] = xt_ref[e, pack * COARSE:(pack + 1) * COARSE, :]
    for at in range(0, far_rows, CHUNK):
        mark = jnp.where(ftile[0, at:at + CHUNK, :].astype(F32)[:, 0:1] > DEAD / 2, MASKED, 0.0)
        bias[NEAR + at:NEAR + at + CHUNK, :] = jnp.broadcast_to(mark, (CHUNK, TOK))

    def fold(value, op):
        return op(value.reshape(CHUNK // 8, 8, TOK), 0)

    for head in range(HEADS):
        lane = slice(head * HEAD_DIM, (head + 1) * HEAD_DIM)
        q = q_ref[:, lane]
        c = c_ref[:, lane]
        fk = ftile.at[head]
        fv = ftile.at[HEADS + head]
        score[head, NEAR:, :] = dot(fk[...], q, NT)
        dp[head, NEAR:, :] = dot(fv[...], c, NT)
        top = jnp.full((8, TOK), MASKED, F32)
        for at in range(0, NEAR + far_rows, CHUNK):
            t = score[head, at:at + CHUNK, :] * SCALE + bias[at:at + CHUNK, :]
            score[head, at:at + CHUNK, :] = t
            top = jnp.maximum(top, fold(t, jnp.max))
        top = jnp.max(top, 0, keepdims=True)
        z = jnp.zeros((8, TOK), F32)
        d = jnp.zeros((8, TOK), F32)
        for at in range(0, NEAR + far_rows, CHUNK):
            e = jnp.exp(score[head, at:at + CHUNK, :] - top)
            score[head, at:at + CHUNK, :] = e
            z = z + fold(e, jnp.sum)
            d = d + fold(e * dp[head, at:at + CHUNK, :], jnp.sum)
        inv = 1.0 / jnp.sum(z, 0, keepdims=True)
        delta = jnp.sum(d, 0, keepdims=True) * inv
        for at in range(0, NEAR + far_rows, CHUNK):
            p = score[head, at:at + CHUNK, :] * inv
            p_t[at:at + CHUNK, :] = p.astype(BF)
            ds_t[at:at + CHUNK, :] = (p * (dp[head, at:at + CHUNK, :] - delta)).astype(BF)
        gk = dot(ds_t[...], q, NN) * SCALE
        gv = dot(p_t[...], c, NN)
        for pack, g in ((head, gk), (HEADS + head, gv)):
            wide = slice(pack * HEAD_DIM, (pack + 1) * HEAD_DIM)
            edge_s[0, :, wide] = g[0:BLOCK].astype(BF)
            own_g[:, wide] = g[BLOCK:3 * BLOCK]
            edge_s[1, :, wide] = g[3 * BLOCK:NEAR].astype(BF)
            for level in range(direct):
                at = NEAR + level * COARSE
                rows = rows_of(level)
                part = g[at:at + COARSE]
                if rows >= 16:
                    for m in range(1 << level):
                        dst = level * TILE + (m * PACK + pack) * rows
                        gsend[dst:dst + rows, :] = part[m * rows:(m + 1) * rows].astype(BF)
                else:
                    small[0:COARSE, :] = part
                    for m in range(1 << level):
                        dst = (m * PACK + pack) * rows
                        mixed_g = mixed if level == 3 else mixed2
                        mixed_g[dst:dst + rows, :] = small[m * rows:(m + 1) * rows, :]
            for e in range(extra):
                at = NEAR + (direct + e) * COARSE
                xg_ref[e, pack * COARSE:(pack + 1) * COARSE, :] = g[at:at + COARSE]
        out = dot(vn[:, lane], p_t[0:NEAR, :], TN) + dot(fv[...], p_t[NEAR:, :], TN)
        att_ref[:, lane] = out.T.astype(BF)
        out = dot(kn[:, lane], ds_t[0:NEAR, :], TN) + dot(fk[...], ds_t[NEAR:, :], TN)
        qg_ref[:, lane] = (out * SCALE).T.astype(BF)

    def edge(side):
        dev = me - 1 if side == 0 else me + 1
        return pltpu.make_async_remote_copy(
            src_ref=edge_s.at[side], dst_ref=edge_r.at[1 - side],
            send_sem=ed_ss.at[side], recv_sem=ed_rs.at[side],
            device_id=where_is(dev), device_id_type=MESH,
        )

    @pl.when(has_prev)
    def _():
        edge(0).start()

    @pl.when(has_next)
    def _():
        edge(1).start()

    for level in reversed(range(direct)):
        if rows_of(level) < 16:
            regrouped = mixed if level == 3 else mixed2
            gsend[level * TILE:(level + 1) * TILE, :] = regrouped[...].astype(BF)
        size = PACK * rows_of(level)
        spread_out(
            level,
            lambda m, at=level * TILE, n=size: gsend.at[pl.ds(pl.multiple_of(at + m * n, n), n), :],
            grecv, dn_ss, dn_rs,
        )

    stores[0].start()
    stores[1].start()
    low_p, size_p = level_row_maps(direct, (TOK, 128), 1)
    pos_p = iota((TOK, 128), 0)
    share = jnp.where(
        (pos_p >= low_p) & (pos_p < low_p + size_p) & (pos_p < count), 1.0, 0.0
    ).astype(BF)
    share = jnp.concatenate([share, share], axis=1)

    gsum[:, row_offset(direct):, :] = jnp.zeros((PACK, 128 - row_offset(direct), 128), F32)
    for level in range(direct):
        whole = grecv.at[level * TILE:(level + 1) * TILE, :]
        pltpu.make_async_copy(whole, whole, dn_rs.at[level]).wait()
        rows = rows_of(level)
        n = PACK * rows
        total = grecv[level * TILE:level * TILE + n, :].astype(F32)
        for m in range(1, 1 << level):
            total = total + grecv[level * TILE + m * n:level * TILE + (m + 1) * n, :].astype(F32)
        at = row_offset(level)
        if rows >= 8:
            for pack in range(PACK):
                gsum[pack, at:at + rows, :] = total[pack * rows:(pack + 1) * rows]
        else:
            small[0:n, :] = total
            for pack in range(PACK):
                gsum[pack, at:at + rows, :] = small[pack * rows:(pack + 1) * rows, :]

    @pl.when(has_next)
    def _():
        edge(0).wait_recv()

    @pl.when(has_prev)
    def _():
        edge(1).wait_recv()

    for pack in range(PACK):
        wide = slice(pack * HEAD_DIM, (pack + 1) * HEAD_DIM)
        lane = slice((pack % HEADS) * HEAD_DIM, (pack % HEADS + 1) * HEAD_DIM)
        g = gsum[pack] / row_div
        high = g.astype(BF)
        rest_g = (g - high.astype(F32)).astype(BF)
        total = own_g[:, wide] + dot(share, jnp.concatenate([high, rest_g], axis=0), NN)
        total = total + jnp.concatenate([edge_r[0, :, wide], edge_r[1, :, wide]], 0).astype(F32)
        out = kg_ref if pack < HEADS else vg_ref
        out[:, lane] = total.astype(out.dtype)
        if pack % HEADS == HEADS - 1:
            stores[2 + pack // HEADS].start()

    @pl.when(has_prev)
    def _():
        halo(0, 0).wait_send()
        halo(1, 0).wait_send()
        edge(0).wait_send()

    @pl.when(has_next)
    def _():
        halo(0, 1).wait_send()
        halo(1, 1).wait_send()
        edge(1).wait_send()

    for level in range(direct):
        whole = far.at[level * TILE:(level + 1) * TILE, :]
        pltpu.make_async_copy(whole, whole, up_ss.at[level]).wait()
        whole = grecv.at[level * TILE:(level + 1) * TILE, :]
        pltpu.make_async_copy(whole, whole, dn_ss.at[level]).wait()
    for store in stores:
        store.wait()


def deliver(*refs):
    sems = refs[8]
    copies = [pltpu.make_async_copy(refs[i], refs[4 + i], sems.at[i]) for i in range(4)]
    for copy in copies:
        copy.start()
    for copy in copies:
        copy.wait()


def swapped(block, axis, stride):
    count = lax.axis_size(axis)
    route = [(i, i ^ (1 << stride)) for i in range(count)]
    return lax.ppermute(block, axis, route)


def halved(lower, upper):
    both = jnp.concatenate([lower, upper], axis=0)
    return both.reshape((both.shape[0] // 2, 2) + both.shape[1:]).sum(axis=1)


def ordered(side, own, other):
    return jnp.where(side == 0, own, other), jnp.where(side == 0, other, own)


def level_axes():
    shard_bits = lax.axis_size("shard").bit_length() - 1
    grp_bits = lax.axis_size("grp").bit_length() - 1
    return [("shard", i) for i in range(shard_bits)] + [("grp", i) for i in range(grp_bits)]


def climb(key_states, value_states, valid_mask, axes, direct):
    mask = valid_mask.astype(F32)
    kv = jnp.concatenate([key_states, value_states], axis=1).astype(F32)
    tile = (kv * mask[:, None]).reshape(COARSE, -1, 2 * WIDTH).sum(axis=1)
    count = mask.reshape(COARSE, -1).sum(axis=1)
    tiles = []
    counts = []
    for level, (axis, bit) in enumerate(axes):
        side = lax.axis_index(axis) >> bit & 1
        other, other_count = swapped((tile, count), axis, bit)
        if level >= direct:
            mean = (other / jnp.maximum(other_count, 1.0)[:, None]).astype(BF)
            marked = jnp.where(other_count[:, None] > 0, mean[:, :WIDTH], jnp.asarray(DEAD, BF))
            mean = jnp.concatenate([marked, mean[:, WIDTH:]], axis=1)
            tiles.append(
                mean.reshape(COARSE, PACK, HEAD_DIM).transpose(1, 0, 2).reshape(TILE, HEAD_DIM))
            counts.append(other_count)
        tile = halved(*ordered(side, tile, other))
        count = halved(*ordered(side, count, other_count))
    return jnp.stack(tiles), jnp.stack(counts)


def descend(grads, counts, axes, direct):
    zero = jnp.zeros((COARSE, 2 * WIDTH), F32)
    own = zero
    for level in reversed(range(len(axes))):
        axis, bit = axes[level]
        side = lax.axis_index(axis) >> bit & 1
        wide = jnp.repeat(own, 2, axis=0)
        mine, theirs = ordered(side, wide[:COARSE], wide[COARSE:])
        if level >= direct:
            part = grads[level - direct].reshape(PACK, COARSE, HEAD_DIM).transpose(1, 0, 2)
            part = part.reshape(COARSE, 2 * WIDTH)
            theirs = theirs + part / jnp.maximum(counts[level - direct], 1.0)[:, None]
        own = mine + swapped(theirs, axis, bit)
    return own


def body(query_states, key_states, value_states, valid_mask, attended_grad):
    axes = level_axes()
    n_grp = lax.axis_size("grp")
    n_shard = lax.axis_size("shard")
    direct = min(DIRECT, len(axes))
    extra = len(axes) - direct
    operands = [
        query_states, key_states, value_states, valid_mask.reshape(1, TOK), attended_grad]
    grad_type = F32 if extra else BF
    outs = [jax.ShapeDtypeStruct((TOK, WIDTH), t) for t in (BF, BF, grad_type, grad_type)]
    if extra:
        tiles, counts = climb(key_states, value_states, valid_mask, axes, direct)
        operands.append(tiles)
        outs.append(jax.ShapeDtypeStruct((extra, TILE, HEAD_DIM), F32))
    vmem = pl.BlockSpec(memory_space=pltpu.VMEM)
    hbm = pl.BlockSpec(memory_space=pltpu.HBM)
    dma = pltpu.SemaphoreType.DMA
    all_rows = NEAR + (direct + extra) * COARSE
    results = pl.pallas_call(
        functools.partial(kernel, n_grp, n_shard, direct, extra),
        out_shape=outs,
        in_specs=[hbm] * 5 + [vmem] * (len(operands) - 5),
        out_specs=[hbm] * 4 + [vmem] * (len(outs) - 4),
        scratch_shapes=[
            pltpu.VMEM((TOK, WIDTH), BF),
            pltpu.VMEM((TOK, WIDTH), BF),
            pltpu.VMEM((TOK, WIDTH), grad_type),
            pltpu.VMEM((TOK, WIDTH), grad_type),
            dma((4,)),
            pltpu.VMEM((TOK, WIDTH), BF),
            pltpu.VMEM((TOK, WIDTH), BF),
            pltpu.VMEM((TOK, WIDTH), BF),
            pltpu.VMEM((TOK, WIDTH), BF),
            pltpu.VMEM((1, TOK), jnp.int32),
            dma((5,)),
            pltpu.VMEM((NEAR, WIDTH), BF),
            pltpu.VMEM((NEAR, WIDTH), BF),
            pltpu.VMEM((up_offset(direct), HEAD_DIM), BF),
            pltpu.VMEM((direct * TILE, HEAD_DIM), BF),
            pltpu.VMEM((PACK, (direct + extra) * COARSE, HEAD_DIM), BF),
            pltpu.VMEM((128, HEAD_DIM), F32),
            pltpu.VMEM((TILE, HEAD_DIM), F32),
            pltpu.VMEM((TILE, HEAD_DIM), F32),
            pltpu.VMEM((all_rows, TOK), F32),
            pltpu.VMEM((HEADS, all_rows, TOK), F32),
            pltpu.VMEM((HEADS, all_rows, TOK), F32),
            pltpu.VMEM((all_rows, TOK), BF),
            pltpu.VMEM((all_rows, TOK), BF),
            pltpu.VMEM((TOK, 2 * WIDTH), F32),
            pltpu.VMEM((2, BLOCK, 2 * WIDTH), BF),
            pltpu.VMEM((2, BLOCK, 2 * WIDTH), BF),
            pltpu.VMEM((direct * TILE, HEAD_DIM), BF),
            pltpu.VMEM((direct * TILE, HEAD_DIM), BF),
            pltpu.VMEM((PACK, 128, HEAD_DIM), F32),
            dma((4,)),
            dma((4,)),
            dma((direct,)),
            dma((direct,)),
            dma((2,)),
            dma((2,)),
            dma((direct,)),
            dma((direct,)),
        ],
        compiler_params=pltpu.CompilerParams(
            collective_id=0, has_side_effects=True, vmem_limit_bytes=63 * 1024 * 1024
        ),
    )(*operands)
    if not extra:
        return pl.pallas_call(
            deliver,
            out_shape=outs,
            in_specs=[hbm] * 4,
            out_specs=[hbm] * 4,
            scratch_shapes=[dma((4,))],
            compiler_params=pltpu.CompilerParams(vmem_limit_bytes=63 * 1024 * 1024),
        )(*results)
    attended, query_grad, key_grad, value_grad, grads = results
    own = descend(grads, counts, axes, direct)
    spread = jnp.repeat(own, TOK // COARSE, axis=0) * valid_mask.astype(F32)[:, None]
    return (
        attended,
        query_grad,
        (key_grad + spread[:, :WIDTH]).astype(BF),
        (value_grad + spread[:, WIDTH:]).astype(BF),
    )


def solution(mesh):
    rows = P(("grp", "shard"), None)
    return jax.shard_map(
        body,
        mesh=mesh,
        in_specs=(rows, rows, rows, P(("grp", "shard")), rows),
        out_specs=(rows, rows, rows, rows),
        check_vma=False,
    )
```

```python
import functools

import jax
import jax.numpy as jnp
from jax import lax
from jax.experimental import pallas as pl
from jax.experimental.pallas import tpu as pltpu
from jax.sharding import PartitionSpec as P

HEADS = 4
HEAD_DIM = 128
BLOCK = 128
COARSE = 64
DIRECT = 5
TOK = 256
WIDTH = HEADS * HEAD_DIM
PACK = 2 * HEADS
TILE = PACK * COARSE
HALVES = 2
PART = PACK // HALVES
PART_HEADS = HEADS // HALVES
PART_TILE = PART * COARSE
PART_WIDTH = PART_HEADS * HEAD_DIM
SCALE = HEAD_DIM ** (-0.5)
MASKED = -1e30
DEAD = 1024.0
DEAD_SUM = 65536.0
MESH = pl.DeviceIdType.MESH
BF = jnp.bfloat16
F32 = jnp.float32


def rows_of(level):
    return COARSE >> level


def up_offset(level):
    return sum(PART * rows_of(i) for i in range(level))


def row_offset(level):
    return sum(rows_of(i) for i in range(level))


def iota(shape, dim):
    return lax.broadcasted_iota(jnp.int32, shape, dim)


def dot(a, b, dims):
    return lax.dot_general(a, b, (dims, ((), ())), preferred_element_type=F32)


NN = ((1,), (0,))
NT = ((1,), (1,))
TN = ((0,), (0,))


CHUNK = 64
NEAR = 4 * BLOCK


def level_row_maps(direct, shape, dim):
    idx = iota(shape, dim)
    low = jnp.full(shape, 2 * TOK, jnp.int32)
    size = jnp.ones(shape, jnp.int32)
    for level in range(direct):
        group = 4 << level
        at = row_offset(level)
        inside = (idx >= at) & (idx < at + rows_of(level))
        low = jnp.where(inside, (idx - at) * group, low)
        size = jnp.where(inside, group, size)
    return low, size


def kernel(
    n_grp, n_shard, direct, extra,
    q_in, k_in, v_in, m_in, c_in, *rest,
):
    if extra:
        xt_ref, *outs_hbm, xg_ref = rest[:6]
        rest = rest[6:]
    else:
        outs_hbm = rest[:4]
        rest = rest[4:]
    (att_ref, qg_ref, kg_ref, vg_ref, out_sem, q_ref, k_ref, v_ref, c_ref, m_ref, in_sem, kn, vn, up, far, ftile, small, mixed, mixed2, bias, score, dp,
     p_t, ds_t, own_g, edge_s, edge_r, gsend, grecv, gsum,
     halo_ss, halo_rs, up_ss, up_rs, ed_ss, ed_rs, dn_ss, dn_rs) = rest
    loads = [
        pltpu.make_async_copy(src, dst, in_sem.at[i])
        for i, (src, dst) in enumerate(
            ((k_in, k_ref), (v_in, v_ref), (q_in, q_ref), (c_in, c_ref), (m_in, m_ref)))
    ]
    for load in loads:
        load.start()
    stores = [
        pltpu.make_async_copy(src, dst, out_sem.at[i])
        for i, (src, dst) in enumerate(zip((att_ref, qg_ref, kg_ref, vg_ref), outs_hbm))
    ]
    n_dev = n_grp * n_shard
    me = lax.axis_index("grp") * n_shard + lax.axis_index("shard")
    span = 1 << direct
    far_rows = (direct + extra) * COARSE

    def where_is(dev):
        return (dev // n_shard, dev % n_shard)

    def sibling(level):
        part = me // (1 << level)
        return (part + 1 - 2 * (part % 2)) * (1 << level)

    base = (me // span) * span
    at_low = me == base
    at_high = me == base + span - 1
    has_prev = me > 0
    has_next = me < n_dev - 1
    out_prev = has_prev & at_low
    out_next = has_next & at_high
    barrier = pltpu.get_barrier_semaphore()

    def hello(t, _):
        pl.semaphore_signal(
            barrier, inc=1, device_id=where_is(base + (me - base + t) % span), device_id_type=MESH
        )
        return 0

    lax.fori_loop(1, span, hello, 0)
    if n_dev > span:
        @pl.when(out_prev)
        def _():
            pl.semaphore_signal(barrier, inc=1, device_id=where_is(me - 1), device_id_type=MESH)

        @pl.when(out_next)
        def _():
            pl.semaphore_signal(barrier, inc=1, device_id=where_is(me + 1), device_id_type=MESH)

    loads[0].wait()
    loads[1].wait()
    loads[4].wait()

    count = jnp.sum(m_ref[...], axis=1, keepdims=True)
    live_col = iota((TOK, 1), 0) < count
    kn[BLOCK:BLOCK + TOK, :] = jnp.where(live_col, k_ref[...].astype(F32), DEAD).astype(BF)
    vn[BLOCK:BLOCK + TOK, :] = v_ref[...]
    low, size = level_row_maps(direct, (128, TOK), 0)
    pos = iota((128, TOK), 1)
    pool = jnp.where((pos >= low) & (pos < low + size) & (pos < count), 1.0, 0.0).astype(BF)
    low_c, size_c = level_row_maps(direct, (128, 1), 0)
    row_count = jnp.clip(count - low_c, 0, size_c).astype(F32)
    row_div = jnp.maximum(row_count, 1.0)
    for half, part_pack in [(h, p) for h in range(HALVES) for p in range(PART)]:
        is_key = part_pack < PART_HEADS
        ref = k_ref if is_key else v_ref
        lane = (half * PART_HEADS + part_pack % PART_HEADS) * HEAD_DIM
        mean = dot(pool, ref[:, lane:lane + HEAD_DIM], NN) / row_div
        if is_key:
            mean = jnp.where(row_count > 0, mean, DEAD)
        for level in range(direct):
            rows = rows_of(level)
            part = mean[row_offset(level):row_offset(level) + rows]
            if rows >= 16:
                at = up_offset(level) + part_pack * rows
                up[half, at:at + rows, :] = part.astype(BF)
            else:
                at = up_offset(level) - up_offset(3) + part_pack * rows
                small[at:at + rows, :] = part
        if direct > 3 and part_pack == PART - 1:
            tail = up_offset(direct) - up_offset(3)
            up[half, up_offset(3):up_offset(direct), :] = small[0:tail, :].astype(BF)

    pl.semaphore_wait(barrier, span - 1)
    if n_dev > span:
        @pl.when(out_prev)
        def _():
            pl.semaphore_wait(barrier, 1)

        @pl.when(out_next)
        def _():
            pl.semaphore_wait(barrier, 1)

    def halo(half, which, side):
        ref = kn if which == 0 else vn
        slot = 4 * half + 2 * which + side
        wide = pl.ds(half * PART_WIDTH, PART_WIDTH)
        if side == 0:
            src, dst, dev = pl.ds(BLOCK, BLOCK), pl.ds(3 * BLOCK, BLOCK), me - 1
        else:
            src, dst, dev = pl.ds(2 * BLOCK, BLOCK), pl.ds(0, BLOCK), me + 1
        return pltpu.make_async_remote_copy(
            src_ref=ref.at[src, wide], dst_ref=ref.at[dst, wide],
            send_sem=halo_ss.at[slot], recv_sem=halo_rs.at[slot],
            device_id=where_is(dev), device_id_type=MESH,
        )

    def send_halo(half):
        @pl.when(has_prev)
        def _():
            halo(half, 0, 0).start()
            halo(half, 1, 0).start()

        @pl.when(has_next)
        def _():
            halo(half, 0, 1).start()
            halo(half, 1, 1).start()

    @pl.when(jnp.logical_not(has_prev))
    def _():
        kn[0:BLOCK, :] = jnp.full((BLOCK, WIDTH), DEAD, BF)
        vn[0:BLOCK, :] = jnp.zeros((BLOCK, WIDTH), BF)
        edge_r[0] = jnp.zeros((HALVES, BLOCK, WIDTH), BF)

    @pl.when(jnp.logical_not(has_next))
    def _():
        kn[3 * BLOCK:4 * BLOCK, :] = jnp.full((BLOCK, WIDTH), DEAD, BF)
        vn[3 * BLOCK:4 * BLOCK, :] = jnp.zeros((BLOCK, WIDTH), BF)
        edge_r[1] = jnp.zeros((HALVES, BLOCK, WIDTH), BF)

    def tile_at(half, level):
        return (half * direct + level) * PART_TILE

    def tile_ref(ref, half, level):
        return ref.at[tile_at(half, level):tile_at(half, level) + PART_TILE, :]

    def spread_out(half, level, source, target, send_sem, recv_sem):
        size = PART * rows_of(level)
        parts = 1 << level
        to = sibling(level)
        land = pl.multiple_of(tile_at(half, level) + (me % parts) * size, size)

        def send(t, _):
            m = (me + t) % parts
            pltpu.make_async_remote_copy(
                src_ref=source(m), dst_ref=target.at[pl.ds(land, size), :],
                send_sem=send_sem.at[half * direct + level],
                recv_sem=recv_sem.at[half * direct + level],
                device_id=where_is(to + m), device_id_type=MESH,
            ).start()
            return 0

        if parts == 1:
            send(0, 0)
        else:
            lax.fori_loop(0, parts, send, 0)

    for half in range(HALVES):
        send_halo(half)
        for level in reversed(range(direct)):
            at = up_offset(level)
            spread_out(
                half, level,
                lambda m, half=half, at=at, n=PART * rows_of(level): up.at[half, at:at + n, :],
                far, up_ss, up_rs,
            )

    loads[2].wait()
    loads[3].wait()
    block_col = iota((1, TOK), 1) // BLOCK

    def near_part(half):
        @pl.when(has_next)
        def _():
            halo(half, 0, 0).wait_recv()
            halo(half, 1, 0).wait_recv()

        @pl.when(has_prev)
        def _():
            halo(half, 0, 1).wait_recv()
            halo(half, 1, 1).wait_recv()

        for at in range(0, NEAR if half == 0 else 0, CHUNK):
            mark = jnp.where(
                kn[at:at + CHUNK, 0:HEAD_DIM].astype(F32)[:, 0:1] > DEAD / 2, MASKED, 0.0)
            mark = jnp.broadcast_to(mark, (CHUNK, TOK))
            if at < BLOCK:
                mark = jnp.where(block_col == 0, mark, MASKED)
            if at >= 3 * BLOCK:
                mark = jnp.where(block_col == 1, mark, MASKED)
            bias[at:at + CHUNK, :] = mark
        for head in range(half * PART_HEADS, (half + 1) * PART_HEADS):
            lane = slice(head * HEAD_DIM, (head + 1) * HEAD_DIM)
            score[head, 0:NEAR, :] = dot(kn[:, lane], q_ref[:, lane], NT)
            dp[head, 0:NEAR, :] = dot(vn[:, lane], c_ref[:, lane], NT)

    def pack_of(half, part_pack):
        head = half * PART_HEADS + part_pack % PART_HEADS
        return head if part_pack < PART_HEADS else HEADS + head

    def take_far(half):
        for level in range(direct):
            whole = tile_ref(far, half, level)
            pltpu.make_async_copy(whole, whole, up_rs.at[half * direct + level]).wait()
            rows = rows_of(level)
            at = level * COARSE
            if rows < 16:
                mixed[...] = whole[...].astype(F32)
            for part_pack in range(PART):
                pack = pack_of(half, part_pack)
                for m in range(1 << level):
                    src = (m * PART + part_pack) * rows
                    if rows >= 16:
                        src += tile_at(half, level)
                        ftile[pack, at + m * rows:at + (m + 1) * rows, :] = far[src:src + rows, :]
                    else:
                        small[m * rows:(m + 1) * rows, :] = mixed[src:src + rows, :]
                if rows < 16:
                    ftile[pack, at:at + COARSE, :] = small[0:COARSE, :].astype(BF)
        for e in range(extra):
            at = (direct + e) * COARSE
            for part_pack in range(PART):
                pack = pack_of(half, part_pack)
                ftile[pack, at:at + COARSE, :] = xt_ref[e, pack * COARSE:(pack + 1) * COARSE, :]
        for at in range(0, far_rows if half == 0 else 0, CHUNK):
            mark = jnp.where(
                ftile[0, at:at + CHUNK, :].astype(F32)[:, 0:1] > DEAD / 2, MASKED, 0.0)
            bias[NEAR + at:NEAR + at + CHUNK, :] = jnp.broadcast_to(mark, (CHUNK, TOK))

    def fold(value, op):
        return op(value.reshape(CHUNK // 8, 8, TOK), 0)

    def attend(head):
        lane = slice(head * HEAD_DIM, (head + 1) * HEAD_DIM)
        q = q_ref[:, lane]
        c = c_ref[:, lane]
        fk = ftile.at[head]
        fv = ftile.at[HEADS + head]
        score[head, NEAR:, :] = dot(fk[...], q, NT)
        dp[head, NEAR:, :] = dot(fv[...], c, NT)
        top = jnp.full((8, TOK), MASKED, F32)
        for at in range(0, NEAR + far_rows, CHUNK):
            t = score[head, at:at + CHUNK, :] * SCALE + bias[at:at + CHUNK, :]
            score[head, at:at + CHUNK, :] = t
            top = jnp.maximum(top, fold(t, jnp.max))
        top = jnp.max(top, 0, keepdims=True)
        z = jnp.zeros((8, TOK), F32)
        d = jnp.zeros((8, TOK), F32)
        for at in range(0, NEAR + far_rows, CHUNK):
            e = jnp.exp(score[head, at:at + CHUNK, :] - top)
            score[head, at:at + CHUNK, :] = e
            z = z + fold(e, jnp.sum)
            d = d + fold(e * dp[head, at:at + CHUNK, :], jnp.sum)
        inv = 1.0 / jnp.sum(z, 0, keepdims=True)
        delta = jnp.sum(d, 0, keepdims=True) * inv
        for at in range(0, NEAR + far_rows, CHUNK):
            p = score[head, at:at + CHUNK, :] * inv
            p_t[at:at + CHUNK, :] = p.astype(BF)
            ds_t[at:at + CHUNK, :] = (p * (dp[head, at:at + CHUNK, :] - delta)).astype(BF)
        gk = dot(ds_t[...], q, NN) * SCALE
        gv = dot(p_t[...], c, NN)
        half = head // PART_HEADS
        for part_pack, pack, g in (
            (head % PART_HEADS, head, gk), (PART_HEADS + head % PART_HEADS, HEADS + head, gv)
        ):
            wide = slice(pack * HEAD_DIM, (pack + 1) * HEAD_DIM)
            edge_wide = slice(part_pack * HEAD_DIM, (part_pack + 1) * HEAD_DIM)
            edge_s[0, half, :, edge_wide] = g[0:BLOCK].astype(BF)
            own_g[:, wide] = g[BLOCK:3 * BLOCK]
            edge_s[1, half, :, edge_wide] = g[3 * BLOCK:NEAR].astype(BF)
            for level in range(direct):
                at = NEAR + level * COARSE
                rows = rows_of(level)
                part = g[at:at + COARSE]
                if rows < 16:
                    small[0:COARSE, :] = part
                for m in range(1 << level):
                    dst = (m * PART + part_pack) * rows
                    if rows >= 16:
                        dst += tile_at(half, level)
                        gsend[dst:dst + rows, :] = part[m * rows:(m + 1) * rows].astype(BF)
                    else:
                        regrouped = mixed if level == 3 else mixed2
                        regrouped[dst:dst + rows, :] = small[m * rows:(m + 1) * rows, :]
            for e in range(extra):
                at = NEAR + (direct + e) * COARSE
                xg_ref[e, pack * COARSE:(pack + 1) * COARSE, :] = g[at:at + COARSE]
        out = dot(vn[:, lane], p_t[0:NEAR, :], TN) + dot(fv[...], p_t[NEAR:, :], TN)
        att_ref[:, lane] = out.T.astype(BF)
        out = dot(kn[:, lane], ds_t[0:NEAR, :], TN) + dot(fk[...], ds_t[NEAR:, :], TN)
        qg_ref[:, lane] = (out * SCALE).T.astype(BF)

    def edge(half, side):
        dev = me - 1 if side == 0 else me + 1
        return pltpu.make_async_remote_copy(
            src_ref=edge_s.at[side, half], dst_ref=edge_r.at[1 - side, half],
            send_sem=ed_ss.at[2 * half + side], recv_sem=ed_rs.at[2 * half + side],
            device_id=where_is(dev), device_id_type=MESH,
        )

    def send_back(half):
        @pl.when(has_prev)
        def _():
            edge(half, 0).start()

        @pl.when(has_next)
        def _():
            edge(half, 1).start()

        for level in reversed(range(direct)):
            at = tile_at(half, level)
            if rows_of(level) < 16:
                regrouped = mixed if level == 3 else mixed2
                gsend[at:at + PART_TILE, :] = regrouped[...].astype(BF)
            size = PART * rows_of(level)
            spread_out(
                half, level,
                lambda m, at=at, n=size: gsend.at[pl.ds(pl.multiple_of(at + m * n, n), n), :],
                grecv, dn_ss, dn_rs,
            )

    near_part(0)
    for half in range(HALVES):
        take_far(half)
        for head in range(half * PART_HEADS, (half + 1) * PART_HEADS):
            attend(head)
        send_back(half)
        if half + 1 < HALVES:
            near_part(half + 1)

    stores[0].start()
    stores[1].start()
    low_p, size_p = level_row_maps(direct, (TOK, 128), 1)
    pos_p = iota((TOK, 128), 0)
    share = jnp.where(
        (pos_p >= low_p) & (pos_p < low_p + size_p) & (pos_p < count), 1.0, 0.0
    ).astype(BF)
    share = jnp.concatenate([share, share], axis=1)

    gsum[:, row_offset(direct):, :] = jnp.zeros((PACK, 128 - row_offset(direct), 128), F32)
    for half in range(HALVES):
        for level in range(direct):
            whole = tile_ref(grecv, half, level)
            pltpu.make_async_copy(whole, whole, dn_rs.at[half * direct + level]).wait()
            rows = rows_of(level)
            n = PART * rows
            at = tile_at(half, level)
            total = grecv[at:at + n, :].astype(F32)
            for m in range(1, 1 << level):
                total = total + grecv[at + m * n:at + (m + 1) * n, :].astype(F32)
            at = row_offset(level)
            if rows < 8:
                small[0:n, :] = total
            for part_pack in range(PART):
                cut = slice(part_pack * rows, (part_pack + 1) * rows)
                pack = pack_of(half, part_pack)
                gsum[pack, at:at + rows, :] = total[cut] if rows >= 8 else small[cut, :]

        @pl.when(has_next)
        def _():
            edge(half, 0).wait_recv()

        @pl.when(has_prev)
        def _():
            edge(half, 1).wait_recv()

        for part_pack in range(PART):
            pack = pack_of(half, part_pack)
            wide = slice(pack * HEAD_DIM, (pack + 1) * HEAD_DIM)
            lane = slice((pack % HEADS) * HEAD_DIM, (pack % HEADS + 1) * HEAD_DIM)
            cut = slice(part_pack * HEAD_DIM, (part_pack + 1) * HEAD_DIM)
            g = gsum[pack] / row_div
            high = g.astype(BF)
            rest_g = (g - high.astype(F32)).astype(BF)
            total = own_g[:, wide] + dot(share, jnp.concatenate([high, rest_g], axis=0), NN)
            total = total + jnp.concatenate(
                [edge_r[0, half, :, cut], edge_r[1, half, :, cut]], 0).astype(F32)
            out = kg_ref if pack < HEADS else vg_ref
            out[:, lane] = total.astype(out.dtype)
    stores[2].start()
    stores[3].start()

    for half in range(HALVES):
        @pl.when(has_prev)
        def _():
            halo(half, 0, 0).wait_send()
            halo(half, 1, 0).wait_send()
            edge(half, 0).wait_send()

        @pl.when(has_next)
        def _():
            halo(half, 0, 1).wait_send()
            halo(half, 1, 1).wait_send()
            edge(half, 1).wait_send()

        for level in range(direct):
            whole = tile_ref(far, half, level)
            pltpu.make_async_copy(whole, whole, up_ss.at[half * direct + level]).wait()
            whole = tile_ref(grecv, half, level)
            pltpu.make_async_copy(whole, whole, dn_ss.at[half * direct + level]).wait()
    for store in stores:
        store.wait()


def deliver(*refs):
    held, in_sem, out_sem = refs[8:]
    ins = [pltpu.make_async_copy(refs[i], held.at[i], in_sem.at[i]) for i in range(4)]
    outs = [pltpu.make_async_copy(held.at[i], refs[4 + i], out_sem.at[i]) for i in range(4)]
    for copy in ins:
        copy.start()
    for i in range(4):
        ins[i].wait()
        outs[i].start()
    for copy in outs:
        copy.wait()


def swapped(block, axis, stride):
    count = lax.axis_size(axis)
    route = [(i, i ^ (1 << stride)) for i in range(count)]
    return lax.ppermute(block, axis, route)


def halved(lower, upper):
    both = jnp.concatenate([lower, upper], axis=0)
    return both.reshape((both.shape[0] // 2, 2) + both.shape[1:]).sum(axis=1)


def ordered(side, own, other):
    return jnp.where(side == 0, own, other), jnp.where(side == 0, other, own)


def level_axes():
    shard_bits = lax.axis_size("shard").bit_length() - 1
    grp_bits = lax.axis_size("grp").bit_length() - 1
    return [("shard", i) for i in range(shard_bits)] + [("grp", i) for i in range(grp_bits)]


def climb(key_states, value_states, valid_mask, axes, direct):
    mask = valid_mask.astype(F32)
    kv = jnp.concatenate([key_states, value_states], axis=1).astype(F32)
    tile = (kv * mask[:, None]).reshape(COARSE, -1, 2 * WIDTH).sum(axis=1)
    count = mask.reshape(COARSE, -1).sum(axis=1)
    tiles = []
    counts = []
    for level, (axis, bit) in enumerate(axes):
        side = lax.axis_index(axis) >> bit & 1
        other, other_count = swapped((tile, count), axis, bit)
        if level >= direct:
            mean = (other / jnp.maximum(other_count, 1.0)[:, None]).astype(BF)
            marked = jnp.where(other_count[:, None] > 0, mean[:, :WIDTH], jnp.asarray(DEAD, BF))
            mean = jnp.concatenate([marked, mean[:, WIDTH:]], axis=1)
            tiles.append(
                mean.reshape(COARSE, PACK, HEAD_DIM).transpose(1, 0, 2).reshape(TILE, HEAD_DIM))
            counts.append(other_count)
        tile = halved(*ordered(side, tile, other))
        count = halved(*ordered(side, count, other_count))
    return jnp.stack(tiles), jnp.stack(counts)


def descend(grads, counts, axes, direct):
    zero = jnp.zeros((COARSE, 2 * WIDTH), F32)
    own = zero
    for level in reversed(range(len(axes))):
        axis, bit = axes[level]
        side = lax.axis_index(axis) >> bit & 1
        wide = jnp.repeat(own, 2, axis=0)
        mine, theirs = ordered(side, wide[:COARSE], wide[COARSE:])
        if level >= direct:
            part = grads[level - direct].reshape(PACK, COARSE, HEAD_DIM).transpose(1, 0, 2)
            part = part.reshape(COARSE, 2 * WIDTH)
            theirs = theirs + part / jnp.maximum(counts[level - direct], 1.0)[:, None]
        own = mine + swapped(theirs, axis, bit)
    return own


def body(query_states, key_states, value_states, valid_mask, attended_grad):
    axes = level_axes()
    n_grp = lax.axis_size("grp")
    n_shard = lax.axis_size("shard")
    direct = min(DIRECT, len(axes))
    extra = len(axes) - direct
    operands = [
        query_states, key_states, value_states, valid_mask.reshape(1, TOK), attended_grad]
    grad_type = F32 if extra else BF
    outs = [jax.ShapeDtypeStruct((TOK, WIDTH), t) for t in (BF, BF, grad_type, grad_type)]
    if extra:
        tiles, counts = climb(key_states, value_states, valid_mask, axes, direct)
        operands.append(tiles)
        outs.append(jax.ShapeDtypeStruct((extra, TILE, HEAD_DIM), F32))
    vmem = pl.BlockSpec(memory_space=pltpu.VMEM)
    hbm = pl.BlockSpec(memory_space=pltpu.HBM)
    dma = pltpu.SemaphoreType.DMA
    all_rows = NEAR + (direct + extra) * COARSE
    results = pl.pallas_call(
        functools.partial(kernel, n_grp, n_shard, direct, extra),
        out_shape=outs,
        in_specs=[hbm] * 5 + [vmem] * (len(operands) - 5),
        out_specs=[hbm] * 4 + [vmem] * (len(outs) - 4),
        scratch_shapes=[
            pltpu.VMEM((TOK, WIDTH), BF),
            pltpu.VMEM((TOK, WIDTH), BF),
            pltpu.VMEM((TOK, WIDTH), grad_type),
            pltpu.VMEM((TOK, WIDTH), grad_type),
            dma((4,)),
            pltpu.VMEM((TOK, WIDTH), BF),
            pltpu.VMEM((TOK, WIDTH), BF),
            pltpu.VMEM((TOK, WIDTH), BF),
            pltpu.VMEM((TOK, WIDTH), BF),
            pltpu.VMEM((1, TOK), jnp.int32),
            dma((5,)),
            pltpu.VMEM((NEAR, WIDTH), BF),
            pltpu.VMEM((NEAR, WIDTH), BF),
            pltpu.VMEM((HALVES, up_offset(direct), HEAD_DIM), BF),
            pltpu.VMEM((direct * TILE, HEAD_DIM), BF),
            pltpu.VMEM((PACK, (direct + extra) * COARSE, HEAD_DIM), BF),
            pltpu.VMEM((128, HEAD_DIM), F32),
            pltpu.VMEM((PART_TILE, HEAD_DIM), F32),
            pltpu.VMEM((PART_TILE, HEAD_DIM), F32),
            pltpu.VMEM((all_rows, TOK), F32),
            pltpu.VMEM((HEADS, all_rows, TOK), F32),
            pltpu.VMEM((HEADS, all_rows, TOK), F32),
            pltpu.VMEM((all_rows, TOK), BF),
            pltpu.VMEM((all_rows, TOK), BF),
            pltpu.VMEM((TOK, 2 * WIDTH), F32),
            pltpu.VMEM((2, HALVES, BLOCK, WIDTH), BF),
            pltpu.VMEM((2, HALVES, BLOCK, WIDTH), BF),
            pltpu.VMEM((direct * TILE, HEAD_DIM), BF),
            pltpu.VMEM((direct * TILE, HEAD_DIM), BF),
            pltpu.VMEM((PACK, 128, HEAD_DIM), F32),
            dma((4 * HALVES,)),
            dma((4 * HALVES,)),
            dma((HALVES * direct,)),
            dma((HALVES * direct,)),
            dma((2 * HALVES,)),
            dma((2 * HALVES,)),
            dma((HALVES * direct,)),
            dma((HALVES * direct,)),
        ],
        compiler_params=pltpu.CompilerParams(
            collective_id=0, has_side_effects=True, vmem_limit_bytes=63 * 1024 * 1024
        ),
    )(*operands)
    if not extra:
        return pl.pallas_call(
            deliver,
            out_shape=outs,
            in_specs=[hbm] * 4,
            out_specs=[hbm] * 4,
            scratch_shapes=[pltpu.VMEM((4, TOK, WIDTH), BF), dma((4,)), dma((4,))],
            compiler_params=pltpu.CompilerParams(vmem_limit_bytes=63 * 1024 * 1024),
        )(*results)
    attended, query_grad, key_grad, value_grad, grads = results
    own = descend(grads, counts, axes, direct)
    spread = jnp.repeat(own, TOK // COARSE, axis=0) * valid_mask.astype(F32)[:, None]
    return (
        attended,
        query_grad,
        (key_grad + spread[:, :WIDTH]).astype(BF),
        (value_grad + spread[:, WIDTH:]).astype(BF),
    )


def solution(mesh):
    rows = P(("grp", "shard"), None)
    return jax.shard_map(
        body,
        mesh=mesh,
        in_specs=(rows, rows, rows, P(("grp", "shard")), rows),
        out_specs=(rows, rows, rows, rows),
        check_vma=False,
    )
```

```python
import functools

import jax
import jax.numpy as jnp
from jax import lax
from jax.experimental import pallas as pl
from jax.experimental.pallas import tpu as pltpu
from jax.sharding import PartitionSpec as P

HEADS = 4
HEAD_DIM = 128
BLOCK = 128
COARSE = 64
DIRECT = 5
TOK = 256
WIDTH = HEADS * HEAD_DIM
PACK = 2 * HEADS
TILE = PACK * COARSE
HALVES = 2
PART = PACK // HALVES
PART_HEADS = HEADS // HALVES
PART_TILE = PART * COARSE
PART_WIDTH = PART_HEADS * HEAD_DIM
SCALE = HEAD_DIM ** (-0.5)
MASKED = -1e30
DEAD = 1024.0
DEAD_SUM = 65536.0
MESH = pl.DeviceIdType.MESH
BF = jnp.bfloat16
F32 = jnp.float32


def rows_of(level):
    return COARSE >> level


def up_offset(level):
    return sum(PART * rows_of(i) for i in range(level))


def row_offset(level):
    return sum(rows_of(i) for i in range(level))


def iota(shape, dim):
    return lax.broadcasted_iota(jnp.int32, shape, dim)


def dot(a, b, dims):
    return lax.dot_general(a, b, (dims, ((), ())), preferred_element_type=F32)


NN = ((1,), (0,))
NT = ((1,), (1,))
TN = ((0,), (0,))


CHUNK = 64
NEAR = 4 * BLOCK


def level_row_maps(direct, shape, dim):
    idx = iota(shape, dim)
    low = jnp.full(shape, 2 * TOK, jnp.int32)
    size = jnp.ones(shape, jnp.int32)
    for level in range(direct):
        group = 4 << level
        at = row_offset(level)
        inside = (idx >= at) & (idx < at + rows_of(level))
        low = jnp.where(inside, (idx - at) * group, low)
        size = jnp.where(inside, group, size)
    return low, size


def kernel(
    n_grp, n_shard, direct, extra,
    q_in, k_in, v_in, m_in, c_in, *rest,
):
    if extra:
        xt_ref, *outs_hbm, xg_ref = rest[:6]
        rest = rest[6:]
    else:
        outs_hbm = rest[:4]
        rest = rest[4:]
    (att_ref, qg_ref, kg_ref, vg_ref, out_sem, q_ref, k_ref, v_ref, c_ref, m_ref, in_sem, kn, vn, up, far, ftile, small, mixed, mixed2, bias, score, dp,
     p_t, ds_t, own_g, edge_s, edge_r, gsend, grecv, gsum,
     halo_ss, halo_rs, hop_ss, hop_rs, up_ss, up_rs, ed_ss, ed_rs, dn_ss, dn_rs) = rest
    loads = [
        pltpu.make_async_copy(src, dst, in_sem.at[i])
        for i, (src, dst) in enumerate(
            ((k_in, k_ref), (v_in, v_ref), (q_in, q_ref), (c_in, c_ref), (m_in, m_ref)))
    ]
    for load in loads:
        load.start()
    stores = [
        pltpu.make_async_copy(src, dst, out_sem.at[i])
        for i, (src, dst) in enumerate(zip((att_ref, qg_ref, kg_ref, vg_ref), outs_hbm))
    ]
    n_dev = n_grp * n_shard
    me = lax.axis_index("grp") * n_shard + lax.axis_index("shard")
    span = 1 << direct
    far_rows = (direct + extra) * COARSE

    def where_is(dev):
        return (dev // n_shard, dev % n_shard)

    def sibling(level):
        part = me // (1 << level)
        return (part + 1 - 2 * (part % 2)) * (1 << level)

    base = (me // span) * span
    at_low = me == base
    at_high = me == base + span - 1
    has_prev = me > 0
    has_next = me < n_dev - 1
    out_prev = has_prev & at_low
    out_next = has_next & at_high
    barrier = pltpu.get_barrier_semaphore()

    def hello(t, _):
        pl.semaphore_signal(
            barrier, inc=1, device_id=where_is(base + (me - base + t) % span), device_id_type=MESH
        )
        return 0

    lax.fori_loop(1, span, hello, 0)
    if n_dev > span:
        @pl.when(out_prev)
        def _():
            pl.semaphore_signal(barrier, inc=1, device_id=where_is(me - 1), device_id_type=MESH)

        @pl.when(out_next)
        def _():
            pl.semaphore_signal(barrier, inc=1, device_id=where_is(me + 1), device_id_type=MESH)

    loads[0].wait()
    loads[1].wait()
    loads[4].wait()

    count = jnp.sum(m_ref[...], axis=1, keepdims=True)
    live_col = iota((TOK, 1), 0) < count
    kn[BLOCK:BLOCK + TOK, :] = jnp.where(live_col, k_ref[...].astype(F32), DEAD).astype(BF)
    vn[BLOCK:BLOCK + TOK, :] = v_ref[...]
    low, size = level_row_maps(direct, (128, TOK), 0)
    pos = iota((128, TOK), 1)
    pool = jnp.where((pos >= low) & (pos < low + size) & (pos < count), 1.0, 0.0).astype(BF)
    low_c, size_c = level_row_maps(direct, (128, 1), 0)
    row_count = jnp.clip(count - low_c, 0, size_c).astype(F32)
    row_div = jnp.maximum(row_count, 1.0)
    for half, part_pack in [(h, p) for h in range(HALVES) for p in range(PART)]:
        is_key = part_pack < PART_HEADS
        ref = k_ref if is_key else v_ref
        lane = (half * PART_HEADS + part_pack % PART_HEADS) * HEAD_DIM
        mean = dot(pool, ref[:, lane:lane + HEAD_DIM], NN) / row_div
        if is_key:
            mean = jnp.where(row_count > 0, mean, DEAD)
        for level in range(direct):
            rows = rows_of(level)
            part = mean[row_offset(level):row_offset(level) + rows]
            if rows >= 16:
                at = up_offset(level) + part_pack * rows
                up[half, at:at + rows, :] = part.astype(BF)
            else:
                at = up_offset(level) - up_offset(3) + part_pack * rows
                small[at:at + rows, :] = part
        if direct > 3 and part_pack == PART - 1:
            tail = up_offset(direct) - up_offset(3)
            up[half, up_offset(3):up_offset(direct), :] = small[0:tail, :].astype(BF)

    pl.semaphore_wait(barrier, span - 1)
    if n_dev > span:
        @pl.when(out_prev)
        def _():
            pl.semaphore_wait(barrier, 1)

        @pl.when(out_next)
        def _():
            pl.semaphore_wait(barrier, 1)

    def halo(half, which, side):
        ref = kn if which == 0 else vn
        slot = 4 * half + 2 * which + side
        wide = pl.ds(half * PART_WIDTH, PART_WIDTH)
        if side == 0:
            src, dst, dev = pl.ds(BLOCK, BLOCK), pl.ds(3 * BLOCK, BLOCK), me - 1
        else:
            src, dst, dev = pl.ds(2 * BLOCK, BLOCK), pl.ds(0, BLOCK), me + 1
        return pltpu.make_async_remote_copy(
            src_ref=ref.at[src, wide], dst_ref=ref.at[dst, wide],
            send_sem=halo_ss.at[slot], recv_sem=halo_rs.at[slot],
            device_id=where_is(dev), device_id_type=MESH,
        )

    def send_halo(half):
        @pl.when(has_prev)
        def _():
            halo(half, 0, 0).start()
            halo(half, 1, 0).start()

        @pl.when(has_next)
        def _():
            halo(half, 0, 1).start()
            halo(half, 1, 1).start()

    @pl.when(jnp.logical_not(has_prev))
    def _():
        kn[0:BLOCK, :] = jnp.full((BLOCK, WIDTH), DEAD, BF)
        vn[0:BLOCK, :] = jnp.zeros((BLOCK, WIDTH), BF)
        edge_r[0] = jnp.zeros((HALVES, BLOCK, WIDTH), BF)

    @pl.when(jnp.logical_not(has_next))
    def _():
        kn[3 * BLOCK:4 * BLOCK, :] = jnp.full((BLOCK, WIDTH), DEAD, BF)
        vn[3 * BLOCK:4 * BLOCK, :] = jnp.zeros((BLOCK, WIDTH), BF)
        edge_r[1] = jnp.zeros((HALVES, BLOCK, WIDTH), BF)

    def tile_at(half, level):
        return (half * direct + level) * PART_TILE

    def tile_ref(ref, half, level):
        return ref.at[tile_at(half, level):tile_at(half, level) + PART_TILE, :]

    def spread_out(half, level, source, target, send_sem, recv_sem):
        size = PART * rows_of(level)
        parts = 1 << level
        to = sibling(level)
        land = pl.multiple_of(tile_at(half, level) + (me % parts) * size, size)

        def send(t, _):
            m = (me + t) % parts
            pltpu.make_async_remote_copy(
                src_ref=source(m), dst_ref=target.at[pl.ds(land, size), :],
                send_sem=send_sem.at[half * direct + level],
                recv_sem=recv_sem.at[half * direct + level],
                device_id=where_is(to + m), device_id_type=MESH,
            ).start()
            return 0

        if parts == 1:
            send(0, 0)
        else:
            lax.fori_loop(0, parts, send, 0)

    def first_hop(half, level):
        size = PART * rows_of(level)
        parts = 1 << level
        fours = parts // 4
        at = up_offset(level)
        to = sibling(level)
        land = pl.multiple_of(tile_at(half, level) + (me % parts) * size, size)

        def send(t, _):
            m = me % 4 + 4 * ((me // 4 + t) % fours)
            pltpu.make_async_remote_copy(
                src_ref=up.at[half, at:at + size, :], dst_ref=far.at[pl.ds(land, size), :],
                send_sem=hop_ss.at[half * direct + level],
                recv_sem=hop_rs.at[half * direct + level],
                device_id=where_is(to + m), device_id_type=MESH,
            ).start()
            return 0

        lax.fori_loop(0, fours, send, 0)

    def second_hop(half):
        for level in reversed(range(2, direct)):
            size = PART * rows_of(level)
            at = tile_at(half, level)
            whole = far.at[at:at + PART_TILE // 4, :]
            pltpu.make_async_copy(whole, whole, hop_rs.at[half * direct + level]).wait()

            def send(t, _):
                land = pl.multiple_of(at + (me % 4 + 4 * (t // 3)) * size, size)
                pltpu.make_async_remote_copy(
                    src_ref=far.at[pl.ds(land, size), :], dst_ref=far.at[pl.ds(land, size), :],
                    send_sem=up_ss.at[half * direct + level],
                    recv_sem=up_rs.at[half * direct + level],
                    device_id=where_is((me // 4) * 4 + (me + 1 + t % 3) % 4),
                    device_id_type=MESH,
                ).start()
                return 0

            lax.fori_loop(0, 3 * ((1 << level) // 4), send, 0)

    def up_ref(half, level):
        at = tile_at(half, level)
        return far.at[at:at + (PART_TILE if level < 2 else 3 * (PART_TILE // 4)), :]

    for half in range(HALVES):
        for level in reversed(range(2, direct)):
            first_hop(half, level)
        send_halo(half)
        for level in reversed(range(min(2, direct))):
            at = up_offset(level)
            spread_out(
                half, level,
                lambda m, half=half, at=at, n=PART * rows_of(level): up.at[half, at:at + n, :],
                far, up_ss, up_rs,
            )

    loads[2].wait()
    loads[3].wait()
    block_col = iota((1, TOK), 1) // BLOCK

    def near_part(half):
        @pl.when(has_next)
        def _():
            halo(half, 0, 0).wait_recv()
            halo(half, 1, 0).wait_recv()

        @pl.when(has_prev)
        def _():
            halo(half, 0, 1).wait_recv()
            halo(half, 1, 1).wait_recv()

        for at in range(0, NEAR if half == 0 else 0, CHUNK):
            mark = jnp.where(
                kn[at:at + CHUNK, 0:HEAD_DIM].astype(F32)[:, 0:1] > DEAD / 2, MASKED, 0.0)
            mark = jnp.broadcast_to(mark, (CHUNK, TOK))
            if at < BLOCK:
                mark = jnp.where(block_col == 0, mark, MASKED)
            if at >= 3 * BLOCK:
                mark = jnp.where(block_col == 1, mark, MASKED)
            bias[at:at + CHUNK, :] = mark
        for head in range(half * PART_HEADS, (half + 1) * PART_HEADS):
            lane = slice(head * HEAD_DIM, (head + 1) * HEAD_DIM)
            score[head, 0:NEAR, :] = dot(kn[:, lane], q_ref[:, lane], NT)
            dp[head, 0:NEAR, :] = dot(vn[:, lane], c_ref[:, lane], NT)

    def pack_of(half, part_pack):
        head = half * PART_HEADS + part_pack % PART_HEADS
        return head if part_pack < PART_HEADS else HEADS + head

    def take_far(half):
        for level in range(direct):
            landed = up_ref(half, level)
            pltpu.make_async_copy(landed, landed, up_rs.at[half * direct + level]).wait()
            whole = tile_ref(far, half, level)
            rows = rows_of(level)
            at = level * COARSE
            if rows < 16:
                mixed[...] = whole[...].astype(F32)
            for part_pack in range(PART):
                pack = pack_of(half, part_pack)
                for m in range(1 << level):
                    src = (m * PART + part_pack) * rows
                    if rows >= 16:
                        src += tile_at(half, level)
                        ftile[pack, at + m * rows:at + (m + 1) * rows, :] = far[src:src + rows, :]
                    else:
                        small[m * rows:(m + 1) * rows, :] = mixed[src:src + rows, :]
                if rows < 16:
                    ftile[pack, at:at + COARSE, :] = small[0:COARSE, :].astype(BF)
        for e in range(extra):
            at = (direct + e) * COARSE
            for part_pack in range(PART):
                pack = pack_of(half, part_pack)
                ftile[pack, at:at + COARSE, :] = xt_ref[e, pack * COARSE:(pack + 1) * COARSE, :]
        for at in range(0, far_rows if half == 0 else 0, CHUNK):
            mark = jnp.where(
                ftile[0, at:at + CHUNK, :].astype(F32)[:, 0:1] > DEAD / 2, MASKED, 0.0)
            bias[NEAR + at:NEAR + at + CHUNK, :] = jnp.broadcast_to(mark, (CHUNK, TOK))

    def fold(value, op):
        return op(value.reshape(CHUNK // 8, 8, TOK), 0)

    def attend(head):
        lane = slice(head * HEAD_DIM, (head + 1) * HEAD_DIM)
        q = q_ref[:, lane]
        c = c_ref[:, lane]
        fk = ftile.at[head]
        fv = ftile.at[HEADS + head]
        score[head, NEAR:, :] = dot(fk[...], q, NT)
        dp[head, NEAR:, :] = dot(fv[...], c, NT)
        top = jnp.full((8, TOK), MASKED, F32)
        for at in range(0, NEAR + far_rows, CHUNK):
            t = score[head, at:at + CHUNK, :] * SCALE + bias[at:at + CHUNK, :]
            score[head, at:at + CHUNK, :] = t
            top = jnp.maximum(top, fold(t, jnp.max))
        top = jnp.max(top, 0, keepdims=True)
        z = jnp.zeros((8, TOK), F32)
        d = jnp.zeros((8, TOK), F32)
        for at in range(0, NEAR + far_rows, CHUNK):
            e = jnp.exp(score[head, at:at + CHUNK, :] - top)
            score[head, at:at + CHUNK, :] = e
            z = z + fold(e, jnp.sum)
            d = d + fold(e * dp[head, at:at + CHUNK, :], jnp.sum)
        inv = 1.0 / jnp.sum(z, 0, keepdims=True)
        delta = jnp.sum(d, 0, keepdims=True) * inv
        for at in range(0, NEAR + far_rows, CHUNK):
            p = score[head, at:at + CHUNK, :] * inv
            p_t[at:at + CHUNK, :] = p.astype(BF)
            ds_t[at:at + CHUNK, :] = (p * (dp[head, at:at + CHUNK, :] - delta)).astype(BF)
        gk = dot(ds_t[...], q, NN) * SCALE
        gv = dot(p_t[...], c, NN)
        half = head // PART_HEADS
        for part_pack, pack, g in (
            (head % PART_HEADS, head, gk), (PART_HEADS + head % PART_HEADS, HEADS + head, gv)
        ):
            wide = slice(pack * HEAD_DIM, (pack + 1) * HEAD_DIM)
            edge_wide = slice(part_pack * HEAD_DIM, (part_pack + 1) * HEAD_DIM)
            edge_s[0, half, :, edge_wide] = g[0:BLOCK].astype(BF)
            own_g[:, wide] = g[BLOCK:3 * BLOCK]
            edge_s[1, half, :, edge_wide] = g[3 * BLOCK:NEAR].astype(BF)
            for level in range(direct):
                at = NEAR + level * COARSE
                rows = rows_of(level)
                part = g[at:at + COARSE]
                if rows < 16:
                    small[0:COARSE, :] = part
                for m in range(1 << level):
                    dst = (m * PART + part_pack) * rows
                    if rows >= 16:
                        dst += tile_at(half, level)
                        gsend[dst:dst + rows, :] = part[m * rows:(m + 1) * rows].astype(BF)
                    else:
                        regrouped = mixed if level == 3 else mixed2
                        regrouped[dst:dst + rows, :] = small[m * rows:(m + 1) * rows, :]
            for e in range(extra):
                at = NEAR + (direct + e) * COARSE
                xg_ref[e, pack * COARSE:(pack + 1) * COARSE, :] = g[at:at + COARSE]
        out = dot(vn[:, lane], p_t[0:NEAR, :], TN) + dot(fv[...], p_t[NEAR:, :], TN)
        att_ref[:, lane] = out.T.astype(BF)
        out = dot(kn[:, lane], ds_t[0:NEAR, :], TN) + dot(fk[...], ds_t[NEAR:, :], TN)
        qg_ref[:, lane] = (out * SCALE).T.astype(BF)

    def edge(half, side):
        dev = me - 1 if side == 0 else me + 1
        return pltpu.make_async_remote_copy(
            src_ref=edge_s.at[side, half], dst_ref=edge_r.at[1 - side, half],
            send_sem=ed_ss.at[2 * half + side], recv_sem=ed_rs.at[2 * half + side],
            device_id=where_is(dev), device_id_type=MESH,
        )

    def send_back(half):
        @pl.when(has_prev)
        def _():
            edge(half, 0).start()

        @pl.when(has_next)
        def _():
            edge(half, 1).start()

        for level in reversed(range(direct)):
            at = tile_at(half, level)
            if rows_of(level) < 16:
                regrouped = mixed if level == 3 else mixed2
                gsend[at:at + PART_TILE, :] = regrouped[...].astype(BF)
            size = PART * rows_of(level)
            spread_out(
                half, level,
                lambda m, at=at, n=size: gsend.at[pl.ds(pl.multiple_of(at + m * n, n), n), :],
                grecv, dn_ss, dn_rs,
            )

    second_hop(0)
    near_part(0)
    second_hop(1)
    for half in range(HALVES):
        take_far(half)
        for head in range(half * PART_HEADS, (half + 1) * PART_HEADS):
            attend(head)
        send_back(half)
        if half + 1 < HALVES:
            near_part(half + 1)

    stores[0].start()
    stores[1].start()
    low_p, size_p = level_row_maps(direct, (TOK, 128), 1)
    pos_p = iota((TOK, 128), 0)
    share = jnp.where(
        (pos_p >= low_p) & (pos_p < low_p + size_p) & (pos_p < count), 1.0, 0.0
    ).astype(BF)
    share = jnp.concatenate([share, share], axis=1)

    gsum[:, row_offset(direct):, :] = jnp.zeros((PACK, 128 - row_offset(direct), 128), F32)
    for half in range(HALVES):
        for level in range(direct):
            whole = tile_ref(grecv, half, level)
            pltpu.make_async_copy(whole, whole, dn_rs.at[half * direct + level]).wait()
            rows = rows_of(level)
            n = PART * rows
            at = tile_at(half, level)
            total = grecv[at:at + n, :].astype(F32)
            for m in range(1, 1 << level):
                total = total + grecv[at + m * n:at + (m + 1) * n, :].astype(F32)
            at = row_offset(level)
            if rows < 8:
                small[0:n, :] = total
            for part_pack in range(PART):
                cut = slice(part_pack * rows, (part_pack + 1) * rows)
                pack = pack_of(half, part_pack)
                gsum[pack, at:at + rows, :] = total[cut] if rows >= 8 else small[cut, :]

        @pl.when(has_next)
        def _():
            edge(half, 0).wait_recv()

        @pl.when(has_prev)
        def _():
            edge(half, 1).wait_recv()

        for part_pack in range(PART):
            pack = pack_of(half, part_pack)
            wide = slice(pack * HEAD_DIM, (pack + 1) * HEAD_DIM)
            lane = slice((pack % HEADS) * HEAD_DIM, (pack % HEADS + 1) * HEAD_DIM)
            cut = slice(part_pack * HEAD_DIM, (part_pack + 1) * HEAD_DIM)
            g = gsum[pack] / row_div
            high = g.astype(BF)
            rest_g = (g - high.astype(F32)).astype(BF)
            total = own_g[:, wide] + dot(share, jnp.concatenate([high, rest_g], axis=0), NN)
            total = total + jnp.concatenate(
                [edge_r[0, half, :, cut], edge_r[1, half, :, cut]], 0).astype(F32)
            out = kg_ref if pack < HEADS else vg_ref
            out[:, lane] = total.astype(out.dtype)
    stores[2].start()
    stores[3].start()

    for half in range(HALVES):
        @pl.when(has_prev)
        def _():
            halo(half, 0, 0).wait_send()
            halo(half, 1, 0).wait_send()
            edge(half, 0).wait_send()

        @pl.when(has_next)
        def _():
            halo(half, 0, 1).wait_send()
            halo(half, 1, 1).wait_send()
            edge(half, 1).wait_send()

        for level in range(direct):
            whole = up_ref(half, level)
            pltpu.make_async_copy(whole, whole, up_ss.at[half * direct + level]).wait()
            if level >= 2:
                whole = far.at[0:PART_TILE // 4, :]
                pltpu.make_async_copy(whole, whole, hop_ss.at[half * direct + level]).wait()
            whole = tile_ref(grecv, half, level)
            pltpu.make_async_copy(whole, whole, dn_ss.at[half * direct + level]).wait()
    for store in stores:
        store.wait()


def deliver(*refs):
    held, in_sem, out_sem = refs[8:]
    ins = [pltpu.make_async_copy(refs[i], held.at[i], in_sem.at[i]) for i in range(4)]
    outs = [pltpu.make_async_copy(held.at[i], refs[4 + i], out_sem.at[i]) for i in range(4)]
    for copy in ins:
        copy.start()
    for i in range(4):
        ins[i].wait()
        outs[i].start()
    for copy in outs:
        copy.wait()


def swapped(block, axis, stride):
    count = lax.axis_size(axis)
    route = [(i, i ^ (1 << stride)) for i in range(count)]
    return lax.ppermute(block, axis, route)


def halved(lower, upper):
    both = jnp.concatenate([lower, upper], axis=0)
    return both.reshape((both.shape[0] // 2, 2) + both.shape[1:]).sum(axis=1)


def ordered(side, own, other):
    return jnp.where(side == 0, own, other), jnp.where(side == 0, other, own)


def level_axes():
    shard_bits = lax.axis_size("shard").bit_length() - 1
    grp_bits = lax.axis_size("grp").bit_length() - 1
    return [("shard", i) for i in range(shard_bits)] + [("grp", i) for i in range(grp_bits)]


def climb(key_states, value_states, valid_mask, axes, direct):
    mask = valid_mask.astype(F32)
    kv = jnp.concatenate([key_states, value_states], axis=1).astype(F32)
    tile = (kv * mask[:, None]).reshape(COARSE, -1, 2 * WIDTH).sum(axis=1)
    count = mask.reshape(COARSE, -1).sum(axis=1)
    tiles = []
    counts = []
    for level, (axis, bit) in enumerate(axes):
        side = lax.axis_index(axis) >> bit & 1
        other, other_count = swapped((tile, count), axis, bit)
        if level >= direct:
            mean = (other / jnp.maximum(other_count, 1.0)[:, None]).astype(BF)
            marked = jnp.where(other_count[:, None] > 0, mean[:, :WIDTH], jnp.asarray(DEAD, BF))
            mean = jnp.concatenate([marked, mean[:, WIDTH:]], axis=1)
            tiles.append(
                mean.reshape(COARSE, PACK, HEAD_DIM).transpose(1, 0, 2).reshape(TILE, HEAD_DIM))
            counts.append(other_count)
        tile = halved(*ordered(side, tile, other))
        count = halved(*ordered(side, count, other_count))
    return jnp.stack(tiles), jnp.stack(counts)


def descend(grads, counts, axes, direct):
    zero = jnp.zeros((COARSE, 2 * WIDTH), F32)
    own = zero
    for level in reversed(range(len(axes))):
        axis, bit = axes[level]
        side = lax.axis_index(axis) >> bit & 1
        wide = jnp.repeat(own, 2, axis=0)
        mine, theirs = ordered(side, wide[:COARSE], wide[COARSE:])
        if level >= direct:
            part = grads[level - direct].reshape(PACK, COARSE, HEAD_DIM).transpose(1, 0, 2)
            part = part.reshape(COARSE, 2 * WIDTH)
            theirs = theirs + part / jnp.maximum(counts[level - direct], 1.0)[:, None]
        own = mine + swapped(theirs, axis, bit)
    return own


def body(query_states, key_states, value_states, valid_mask, attended_grad):
    axes = level_axes()
    n_grp = lax.axis_size("grp")
    n_shard = lax.axis_size("shard")
    direct = min(DIRECT, len(axes))
    extra = len(axes) - direct
    operands = [
        query_states, key_states, value_states, valid_mask.reshape(1, TOK), attended_grad]
    grad_type = F32 if extra else BF
    outs = [jax.ShapeDtypeStruct((TOK, WIDTH), t) for t in (BF, BF, grad_type, grad_type)]
    if extra:
        tiles, counts = climb(key_states, value_states, valid_mask, axes, direct)
        operands.append(tiles)
        outs.append(jax.ShapeDtypeStruct((extra, TILE, HEAD_DIM), F32))
    vmem = pl.BlockSpec(memory_space=pltpu.VMEM)
    hbm = pl.BlockSpec(memory_space=pltpu.HBM)
    dma = pltpu.SemaphoreType.DMA
    all_rows = NEAR + (direct + extra) * COARSE
    results = pl.pallas_call(
        functools.partial(kernel, n_grp, n_shard, direct, extra),
        out_shape=outs,
        in_specs=[hbm] * 5 + [vmem] * (len(operands) - 5),
        out_specs=[hbm] * 4 + [vmem] * (len(outs) - 4),
        scratch_shapes=[
            pltpu.VMEM((TOK, WIDTH), BF),
            pltpu.VMEM((TOK, WIDTH), BF),
            pltpu.VMEM((TOK, WIDTH), grad_type),
            pltpu.VMEM((TOK, WIDTH), grad_type),
            dma((4,)),
            pltpu.VMEM((TOK, WIDTH), BF),
            pltpu.VMEM((TOK, WIDTH), BF),
            pltpu.VMEM((TOK, WIDTH), BF),
            pltpu.VMEM((TOK, WIDTH), BF),
            pltpu.VMEM((1, TOK), jnp.int32),
            dma((5,)),
            pltpu.VMEM((NEAR, WIDTH), BF),
            pltpu.VMEM((NEAR, WIDTH), BF),
            pltpu.VMEM((HALVES, up_offset(direct), HEAD_DIM), BF),
            pltpu.VMEM((direct * TILE, HEAD_DIM), BF),
            pltpu.VMEM((PACK, (direct + extra) * COARSE, HEAD_DIM), BF),
            pltpu.VMEM((128, HEAD_DIM), F32),
            pltpu.VMEM((PART_TILE, HEAD_DIM), F32),
            pltpu.VMEM((PART_TILE, HEAD_DIM), F32),
            pltpu.VMEM((all_rows, TOK), F32),
            pltpu.VMEM((HEADS, all_rows, TOK), F32),
            pltpu.VMEM((HEADS, all_rows, TOK), F32),
            pltpu.VMEM((all_rows, TOK), BF),
            pltpu.VMEM((all_rows, TOK), BF),
            pltpu.VMEM((TOK, 2 * WIDTH), F32),
            pltpu.VMEM((2, HALVES, BLOCK, WIDTH), BF),
            pltpu.VMEM((2, HALVES, BLOCK, WIDTH), BF),
            pltpu.VMEM((direct * TILE, HEAD_DIM), BF),
            pltpu.VMEM((direct * TILE, HEAD_DIM), BF),
            pltpu.VMEM((PACK, 128, HEAD_DIM), F32),
            dma((4 * HALVES,)),
            dma((4 * HALVES,)),
            dma((HALVES * direct,)),
            dma((HALVES * direct,)),
            dma((HALVES * direct,)),
            dma((HALVES * direct,)),
            dma((2 * HALVES,)),
            dma((2 * HALVES,)),
            dma((HALVES * direct,)),
            dma((HALVES * direct,)),
        ],
        compiler_params=pltpu.CompilerParams(
            collective_id=0, has_side_effects=True, vmem_limit_bytes=63 * 1024 * 1024
        ),
    )(*operands)
    if not extra:
        return pl.pallas_call(
            deliver,
            out_shape=outs,
            in_specs=[hbm] * 4,
            out_specs=[hbm] * 4,
            scratch_shapes=[pltpu.VMEM((4, TOK, WIDTH), BF), dma((4,)), dma((4,))],
            compiler_params=pltpu.CompilerParams(vmem_limit_bytes=63 * 1024 * 1024),
        )(*results)
    attended, query_grad, key_grad, value_grad, grads = results
    own = descend(grads, counts, axes, direct)
    spread = jnp.repeat(own, TOK // COARSE, axis=0) * valid_mask.astype(F32)[:, None]
    return (
        attended,
        query_grad,
        (key_grad + spread[:, :WIDTH]).astype(BF),
        (value_grad + spread[:, WIDTH:]).astype(BF),
    )


def solution(mesh):
    rows = P(("grp", "shard"), None)
    return jax.shard_map(
        body,
        mesh=mesh,
        in_specs=(rows, rows, rows, P(("grp", "shard")), rows),
        out_specs=(rows, rows, rows, rows),
        check_vma=False,
    )
```

```python
import functools

import jax
import jax.numpy as jnp
from jax import lax
from jax.experimental import pallas as pl
from jax.experimental.pallas import tpu as pltpu
from jax.sharding import PartitionSpec as P

HEADS = 4
HEAD_DIM = 128
BLOCK = 128
COARSE = 64
DIRECT = 5
TOK = 256
WIDTH = HEADS * HEAD_DIM
PACK = 2 * HEADS
TILE = PACK * COARSE
HALVES = 2
PART = PACK // HALVES
PART_HEADS = HEADS // HALVES
PART_TILE = PART * COARSE
PART_WIDTH = PART_HEADS * HEAD_DIM
SCALE = HEAD_DIM ** (-0.5)
MASKED = -1e30
DEAD = 1024.0
DEAD_SUM = 65536.0
MESH = pl.DeviceIdType.MESH
BF = jnp.bfloat16
F32 = jnp.float32


def rows_of(level):
    return COARSE >> level


def up_offset(level):
    return sum(PART * rows_of(i) for i in range(level))


def row_offset(level):
    return sum(rows_of(i) for i in range(level))


def iota(shape, dim):
    return lax.broadcasted_iota(jnp.int32, shape, dim)


def dot(a, b, dims):
    return lax.dot_general(a, b, (dims, ((), ())), preferred_element_type=F32)


NN = ((1,), (0,))
NT = ((1,), (1,))
TN = ((0,), (0,))


CHUNK = 64
NEAR = 4 * BLOCK


def level_row_maps(direct, shape, dim):
    idx = iota(shape, dim)
    low = jnp.full(shape, 2 * TOK, jnp.int32)
    size = jnp.ones(shape, jnp.int32)
    for level in range(direct):
        group = 4 << level
        at = row_offset(level)
        inside = (idx >= at) & (idx < at + rows_of(level))
        low = jnp.where(inside, (idx - at) * group, low)
        size = jnp.where(inside, group, size)
    return low, size


def kernel(
    n_grp, n_shard, direct, extra,
    q_in, k_in, v_in, m_in, c_in, *rest,
):
    if extra:
        xt_ref, *outs_hbm, xg_ref = rest[:6]
        rest = rest[6:]
    else:
        outs_hbm = rest[:4]
        rest = rest[4:]
    (att_ref, qg_ref, kg_ref, vg_ref, out_sem, q_ref, k_ref, v_ref, c_ref, m_ref, in_sem, kn, vn, up, far, ftile, small, mixed, mixed2, bias, score, dp,
     p_t, ds_t, own_g, edge_s, edge_r, gsend, grecv, gsum,
     halo_ss, halo_rs, up_ss, up_rs, ed_ss, ed_rs, dn_ss, dn_rs) = rest
    loads = [
        pltpu.make_async_copy(src, dst, in_sem.at[i])
        for i, (src, dst) in enumerate(
            ((k_in, k_ref), (v_in, v_ref), (q_in, q_ref), (c_in, c_ref), (m_in, m_ref)))
    ]
    for load in loads:
        load.start()
    stores = [
        pltpu.make_async_copy(src, dst, out_sem.at[i])
        for i, (src, dst) in enumerate(zip((att_ref, qg_ref, kg_ref, vg_ref), outs_hbm))
    ]
    n_dev = n_grp * n_shard
    me = lax.axis_index("grp") * n_shard + lax.axis_index("shard")
    span = 1 << direct
    far_rows = (direct + extra) * COARSE

    def where_is(dev):
        return (dev // n_shard, dev % n_shard)

    def sibling(level):
        part = me // (1 << level)
        return (part + 1 - 2 * (part % 2)) * (1 << level)

    base = (me // span) * span
    at_low = me == base
    at_high = me == base + span - 1
    has_prev = me > 0
    has_next = me < n_dev - 1
    out_prev = has_prev & at_low
    out_next = has_next & at_high
    barrier = pltpu.get_barrier_semaphore()

    def hello(t, _):
        pl.semaphore_signal(
            barrier, inc=1, device_id=where_is(base + (me - base + t) % span), device_id_type=MESH
        )
        return 0

    groups = span // n_shard
    my_grp = lax.axis_index("grp")
    my_shard = lax.axis_index("shard")
    if groups:
        low_grp = base // n_shard
        for g in range(groups):
            to_grp = low_grp + lax.rem(my_grp - low_grp + g, groups)

            def hello_grp(t, _):
                pl.semaphore_signal(
                    barrier, inc=1, device_id=(to_grp, lax.rem(my_shard + t, n_shard)),
                    device_id_type=MESH,
                )
                return 0

            lax.fori_loop(0 if g else 1, n_shard, hello_grp, 0)
    else:
        lax.fori_loop(1, span, hello, 0)
    if n_dev > span:
        @pl.when(out_prev)
        def _():
            pl.semaphore_signal(barrier, inc=1, device_id=where_is(me - 1), device_id_type=MESH)

        @pl.when(out_next)
        def _():
            pl.semaphore_signal(barrier, inc=1, device_id=where_is(me + 1), device_id_type=MESH)

    loads[0].wait()
    loads[1].wait()
    loads[4].wait()

    count = jnp.sum(m_ref[...], axis=1, keepdims=True)
    live_col = iota((TOK, 1), 0) < count
    kn[BLOCK:BLOCK + TOK, :] = jnp.where(live_col, k_ref[...].astype(F32), DEAD).astype(BF)
    vn[BLOCK:BLOCK + TOK, :] = v_ref[...]
    low, size = level_row_maps(direct, (128, TOK), 0)
    pos = iota((128, TOK), 1)
    pool = jnp.where((pos >= low) & (pos < low + size) & (pos < count), 1.0, 0.0).astype(BF)
    low_c, size_c = level_row_maps(direct, (128, 1), 0)
    row_count = jnp.clip(count - low_c, 0, size_c).astype(F32)
    row_div = jnp.maximum(row_count, 1.0)
    for half, part_pack in [(h, p) for h in range(HALVES) for p in range(PART)]:
        is_key = part_pack < PART_HEADS
        ref = k_ref if is_key else v_ref
        lane = (half * PART_HEADS + part_pack % PART_HEADS) * HEAD_DIM
        mean = dot(pool, ref[:, lane:lane + HEAD_DIM], NN) / row_div
        if is_key:
            mean = jnp.where(row_count > 0, mean, DEAD)
        for level in range(direct):
            rows = rows_of(level)
            part = mean[row_offset(level):row_offset(level) + rows]
            if rows >= 16:
                at = up_offset(level) + part_pack * rows
                up[half, at:at + rows, :] = part.astype(BF)
            else:
                at = up_offset(level) - up_offset(3) + part_pack * rows
                small[at:at + rows, :] = part
        if direct > 3 and part_pack == PART - 1:
            tail = up_offset(direct) - up_offset(3)
            up[half, up_offset(3):up_offset(direct), :] = small[0:tail, :].astype(BF)

    pl.semaphore_wait(barrier, span - 1)
    if n_dev > span:
        @pl.when(out_prev)
        def _():
            pl.semaphore_wait(barrier, 1)

        @pl.when(out_next)
        def _():
            pl.semaphore_wait(barrier, 1)

    def halo(half, which, side):
        ref = kn if which == 0 else vn
        slot = 4 * half + 2 * which + side
        wide = pl.ds(half * PART_WIDTH, PART_WIDTH)
        if side == 0:
            src, dst, dev = pl.ds(BLOCK, BLOCK), pl.ds(3 * BLOCK, BLOCK), me - 1
        else:
            src, dst, dev = pl.ds(2 * BLOCK, BLOCK), pl.ds(0, BLOCK), me + 1
        return pltpu.make_async_remote_copy(
            src_ref=ref.at[src, wide], dst_ref=ref.at[dst, wide],
            send_sem=halo_ss.at[slot], recv_sem=halo_rs.at[slot],
            device_id=where_is(dev), device_id_type=MESH,
        )

    def send_halo(half):
        @pl.when(has_prev)
        def _():
            halo(half, 0, 0).start()
            halo(half, 1, 0).start()

        @pl.when(has_next)
        def _():
            halo(half, 0, 1).start()
            halo(half, 1, 1).start()

    @pl.when(jnp.logical_not(has_prev))
    def _():
        kn[0:BLOCK, :] = jnp.full((BLOCK, WIDTH), DEAD, BF)
        vn[0:BLOCK, :] = jnp.zeros((BLOCK, WIDTH), BF)
        edge_r[0] = jnp.zeros((HALVES, BLOCK, WIDTH), BF)

    @pl.when(jnp.logical_not(has_next))
    def _():
        kn[3 * BLOCK:4 * BLOCK, :] = jnp.full((BLOCK, WIDTH), DEAD, BF)
        vn[3 * BLOCK:4 * BLOCK, :] = jnp.zeros((BLOCK, WIDTH), BF)
        edge_r[1] = jnp.zeros((HALVES, BLOCK, WIDTH), BF)

    def tile_at(half, level):
        return (half * direct + level) * PART_TILE

    def tile_ref(ref, half, level):
        return ref.at[tile_at(half, level):tile_at(half, level) + PART_TILE, :]

    def spread_out(half, level, source, target, send_sem, recv_sem):
        size = PART * rows_of(level)
        parts = 1 << level
        to_grp, to_shard = where_is(sibling(level))
        ring = min(parts, n_shard)
        first = me % ring
        land = pl.multiple_of(tile_at(half, level) + (me % parts) * size, size)

        def send(g, t, _):
            lane = lax.rem(first + t, ring)
            m = g * n_shard + lane
            pltpu.make_async_remote_copy(
                src_ref=source(m), dst_ref=target.at[pl.ds(land, size), :],
                send_sem=send_sem.at[half * direct + level],
                recv_sem=recv_sem.at[half * direct + level],
                device_id=(to_grp + g, to_shard + lane), device_id_type=MESH,
            ).start()
            return 0

        for g in range(parts // ring):
            if ring == 1:
                send(g, 0, 0)
            else:
                lax.fori_loop(0, ring, functools.partial(send, g), 0)

    for half in range(HALVES):
        send_halo(half)
        for level in reversed(range(direct)):
            at = up_offset(level)
            spread_out(
                half, level,
                lambda m, half=half, at=at, n=PART * rows_of(level): up.at[half, at:at + n, :],
                far, up_ss, up_rs,
            )

    loads[2].wait()
    loads[3].wait()
    block_col = iota((1, TOK), 1) // BLOCK

    def near_part(half):
        @pl.when(has_next)
        def _():
            halo(half, 0, 0).wait_recv()
            halo(half, 1, 0).wait_recv()

        @pl.when(has_prev)
        def _():
            halo(half, 0, 1).wait_recv()
            halo(half, 1, 1).wait_recv()

        for at in range(0, NEAR if half == 0 else 0, CHUNK):
            mark = jnp.where(
                kn[at:at + CHUNK, 0:HEAD_DIM].astype(F32)[:, 0:1] > DEAD / 2, MASKED, 0.0)
            mark = jnp.broadcast_to(mark, (CHUNK, TOK))
            if at < BLOCK:
                mark = jnp.where(block_col == 0, mark, MASKED)
            if at >= 3 * BLOCK:
                mark = jnp.where(block_col == 1, mark, MASKED)
            bias[at:at + CHUNK, :] = mark
        for head in range(half * PART_HEADS, (half + 1) * PART_HEADS):
            lane = slice(head * HEAD_DIM, (head + 1) * HEAD_DIM)
            score[head, 0:NEAR, :] = dot(kn[:, lane], q_ref[:, lane], NT)
            dp[head, 0:NEAR, :] = dot(vn[:, lane], c_ref[:, lane], NT)

    def pack_of(half, part_pack):
        head = half * PART_HEADS + part_pack % PART_HEADS
        return head if part_pack < PART_HEADS else HEADS + head

    def take_far(half):
        for level in range(direct):
            whole = tile_ref(far, half, level)
            pltpu.make_async_copy(whole, whole, up_rs.at[half * direct + level]).wait()
            rows = rows_of(level)
            at = level * COARSE
            if rows < 16:
                mixed[...] = whole[...].astype(F32)
            for part_pack in range(PART):
                pack = pack_of(half, part_pack)
                for m in range(1 << level):
                    src = (m * PART + part_pack) * rows
                    if rows >= 16:
                        src += tile_at(half, level)
                        ftile[pack, at + m * rows:at + (m + 1) * rows, :] = far[src:src + rows, :]
                    else:
                        small[m * rows:(m + 1) * rows, :] = mixed[src:src + rows, :]
                if rows < 16:
                    ftile[pack, at:at + COARSE, :] = small[0:COARSE, :].astype(BF)
        for e in range(extra):
            at = (direct + e) * COARSE
            for part_pack in range(PART):
                pack = pack_of(half, part_pack)
                ftile[pack, at:at + COARSE, :] = xt_ref[e, pack * COARSE:(pack + 1) * COARSE, :]
        for at in range(0, far_rows if half == 0 else 0, CHUNK):
            mark = jnp.where(
                ftile[0, at:at + CHUNK, :].astype(F32)[:, 0:1] > DEAD / 2, MASKED, 0.0)
            bias[NEAR + at:NEAR + at + CHUNK, :] = jnp.broadcast_to(mark, (CHUNK, TOK))

    def fold(value, op):
        return op(value.reshape(CHUNK // 8, 8, TOK), 0)

    def attend(head):
        lane = slice(head * HEAD_DIM, (head + 1) * HEAD_DIM)
        q = q_ref[:, lane]
        c = c_ref[:, lane]
        fk = ftile.at[head]
        fv = ftile.at[HEADS + head]
        score[head, NEAR:, :] = dot(fk[...], q, NT)
        dp[head, NEAR:, :] = dot(fv[...], c, NT)
        top = jnp.full((8, TOK), MASKED, F32)
        for at in range(0, NEAR + far_rows, CHUNK):
            t = score[head, at:at + CHUNK, :] * SCALE + bias[at:at + CHUNK, :]
            score[head, at:at + CHUNK, :] = t
            top = jnp.maximum(top, fold(t, jnp.max))
        top = jnp.max(top, 0, keepdims=True)
        z = jnp.zeros((8, TOK), F32)
        d = jnp.zeros((8, TOK), F32)
        for at in range(0, NEAR + far_rows, CHUNK):
            e = jnp.exp(score[head, at:at + CHUNK, :] - top)
            score[head, at:at + CHUNK, :] = e
            z = z + fold(e, jnp.sum)
            d = d + fold(e * dp[head, at:at + CHUNK, :], jnp.sum)
        inv = 1.0 / jnp.sum(z, 0, keepdims=True)
        delta = jnp.sum(d, 0, keepdims=True) * inv
        for at in range(0, NEAR + far_rows, CHUNK):
            p = score[head, at:at + CHUNK, :] * inv
            p_t[at:at + CHUNK, :] = p.astype(BF)
            ds_t[at:at + CHUNK, :] = (p * (dp[head, at:at + CHUNK, :] - delta)).astype(BF)
        gk = dot(ds_t[...], q, NN) * SCALE
        gv = dot(p_t[...], c, NN)
        half = head // PART_HEADS
        for part_pack, pack, g in (
            (head % PART_HEADS, head, gk), (PART_HEADS + head % PART_HEADS, HEADS + head, gv)
        ):
            wide = slice(pack * HEAD_DIM, (pack + 1) * HEAD_DIM)
            edge_wide = slice(part_pack * HEAD_DIM, (part_pack + 1) * HEAD_DIM)
            edge_s[0, half, :, edge_wide] = g[0:BLOCK].astype(BF)
            own_g[:, wide] = g[BLOCK:3 * BLOCK]
            edge_s[1, half, :, edge_wide] = g[3 * BLOCK:NEAR].astype(BF)
            for level in range(direct):
                at = NEAR + level * COARSE
                rows = rows_of(level)
                part = g[at:at + COARSE]
                if rows < 16:
                    small[0:COARSE, :] = part
                for m in range(1 << level):
                    dst = (m * PART + part_pack) * rows
                    if rows >= 16:
                        dst += tile_at(half, level)
                        gsend[dst:dst + rows, :] = part[m * rows:(m + 1) * rows].astype(BF)
                    else:
                        regrouped = mixed if level == 3 else mixed2
                        regrouped[dst:dst + rows, :] = small[m * rows:(m + 1) * rows, :]
            for e in range(extra):
                at = NEAR + (direct + e) * COARSE
                xg_ref[e, pack * COARSE:(pack + 1) * COARSE, :] = g[at:at + COARSE]
        out = dot(vn[:, lane], p_t[0:NEAR, :], TN) + dot(fv[...], p_t[NEAR:, :], TN)
        att_ref[:, lane] = out.T.astype(BF)
        out = dot(kn[:, lane], ds_t[0:NEAR, :], TN) + dot(fk[...], ds_t[NEAR:, :], TN)
        qg_ref[:, lane] = (out * SCALE).T.astype(BF)

    def edge(half, side):
        dev = me - 1 if side == 0 else me + 1
        return pltpu.make_async_remote_copy(
            src_ref=edge_s.at[side, half], dst_ref=edge_r.at[1 - side, half],
            send_sem=ed_ss.at[2 * half + side], recv_sem=ed_rs.at[2 * half + side],
            device_id=where_is(dev), device_id_type=MESH,
        )

    def send_back(half):
        @pl.when(has_prev)
        def _():
            edge(half, 0).start()

        @pl.when(has_next)
        def _():
            edge(half, 1).start()

        for level in reversed(range(direct)):
            at = tile_at(half, level)
            if rows_of(level) < 16:
                regrouped = mixed if level == 3 else mixed2
                gsend[at:at + PART_TILE, :] = regrouped[...].astype(BF)
            size = PART * rows_of(level)
            spread_out(
                half, level,
                lambda m, at=at, n=size: gsend.at[pl.ds(pl.multiple_of(at + m * n, n), n), :],
                grecv, dn_ss, dn_rs,
            )

    near_part(0)
    for half in range(HALVES):
        take_far(half)
        for head in range(half * PART_HEADS, (half + 1) * PART_HEADS):
            attend(head)
        send_back(half)
        if half + 1 < HALVES:
            near_part(half + 1)

    stores[0].start()
    stores[1].start()
    low_p, size_p = level_row_maps(direct, (TOK, 128), 1)
    pos_p = iota((TOK, 128), 0)
    share = jnp.where(
        (pos_p >= low_p) & (pos_p < low_p + size_p) & (pos_p < count), 1.0, 0.0
    ).astype(BF)
    share = jnp.concatenate([share, share], axis=1)

    gsum[:, row_offset(direct):, :] = jnp.zeros((PACK, 128 - row_offset(direct), 128), F32)
    for half in range(HALVES):
        for level in range(direct):
            whole = tile_ref(grecv, half, level)
            pltpu.make_async_copy(whole, whole, dn_rs.at[half * direct + level]).wait()
            rows = rows_of(level)
            n = PART * rows
            at = tile_at(half, level)
            total = grecv[at:at + n, :].astype(F32)
            for m in range(1, 1 << level):
                total = total + grecv[at + m * n:at + (m + 1) * n, :].astype(F32)
            at = row_offset(level)
            if rows < 8:
                small[0:n, :] = total
            for part_pack in range(PART):
                cut = slice(part_pack * rows, (part_pack + 1) * rows)
                pack = pack_of(half, part_pack)
                gsum[pack, at:at + rows, :] = total[cut] if rows >= 8 else small[cut, :]

        @pl.when(has_next)
        def _():
            edge(half, 0).wait_recv()

        @pl.when(has_prev)
        def _():
            edge(half, 1).wait_recv()

        for part_pack in range(PART):
            pack = pack_of(half, part_pack)
            wide = slice(pack * HEAD_DIM, (pack + 1) * HEAD_DIM)
            lane = slice((pack % HEADS) * HEAD_DIM, (pack % HEADS + 1) * HEAD_DIM)
            cut = slice(part_pack * HEAD_DIM, (part_pack + 1) * HEAD_DIM)
            g = gsum[pack] / row_div
            high = g.astype(BF)
            rest_g = (g - high.astype(F32)).astype(BF)
            total = own_g[:, wide] + dot(share, jnp.concatenate([high, rest_g], axis=0), NN)
            total = total + jnp.concatenate(
                [edge_r[0, half, :, cut], edge_r[1, half, :, cut]], 0).astype(F32)
            out = kg_ref if pack < HEADS else vg_ref
            out[:, lane] = total.astype(out.dtype)
    stores[2].start()
    stores[3].start()

    for half in range(HALVES):
        @pl.when(has_prev)
        def _():
            halo(half, 0, 0).wait_send()
            halo(half, 1, 0).wait_send()
            edge(half, 0).wait_send()

        @pl.when(has_next)
        def _():
            halo(half, 0, 1).wait_send()
            halo(half, 1, 1).wait_send()
            edge(half, 1).wait_send()

        for level in range(direct):
            whole = tile_ref(far, half, level)
            pltpu.make_async_copy(whole, whole, up_ss.at[half * direct + level]).wait()
            whole = tile_ref(grecv, half, level)
            pltpu.make_async_copy(whole, whole, dn_ss.at[half * direct + level]).wait()
    for store in stores:
        store.wait()


def deliver(*refs):
    held, in_sem, out_sem = refs[8:]
    ins = [pltpu.make_async_copy(refs[i], held.at[i], in_sem.at[i]) for i in range(4)]
    outs = [pltpu.make_async_copy(held.at[i], refs[4 + i], out_sem.at[i]) for i in range(4)]
    for copy in ins:
        copy.start()
    for i in range(4):
        ins[i].wait()
        outs[i].start()
    for copy in outs:
        copy.wait()


def swapped(block, axis, stride):
    count = lax.axis_size(axis)
    route = [(i, i ^ (1 << stride)) for i in range(count)]
    return lax.ppermute(block, axis, route)


def halved(lower, upper):
    both = jnp.concatenate([lower, upper], axis=0)
    return both.reshape((both.shape[0] // 2, 2) + both.shape[1:]).sum(axis=1)


def ordered(side, own, other):
    return jnp.where(side == 0, own, other), jnp.where(side == 0, other, own)


def level_axes():
    shard_bits = lax.axis_size("shard").bit_length() - 1
    grp_bits = lax.axis_size("grp").bit_length() - 1
    return [("shard", i) for i in range(shard_bits)] + [("grp", i) for i in range(grp_bits)]


def climb(key_states, value_states, valid_mask, axes, direct):
    mask = valid_mask.astype(F32)
    kv = jnp.concatenate([key_states, value_states], axis=1).astype(F32)
    tile = (kv * mask[:, None]).reshape(COARSE, -1, 2 * WIDTH).sum(axis=1)
    count = mask.reshape(COARSE, -1).sum(axis=1)
    tiles = []
    counts = []
    for level, (axis, bit) in enumerate(axes):
        side = lax.axis_index(axis) >> bit & 1
        other, other_count = swapped((tile, count), axis, bit)
        if level >= direct:
            mean = (other / jnp.maximum(other_count, 1.0)[:, None]).astype(BF)
            marked = jnp.where(other_count[:, None] > 0, mean[:, :WIDTH], jnp.asarray(DEAD, BF))
            mean = jnp.concatenate([marked, mean[:, WIDTH:]], axis=1)
            tiles.append(
                mean.reshape(COARSE, PACK, HEAD_DIM).transpose(1, 0, 2).reshape(TILE, HEAD_DIM))
            counts.append(other_count)
        tile = halved(*ordered(side, tile, other))
        count = halved(*ordered(side, count, other_count))
    return jnp.stack(tiles), jnp.stack(counts)


def descend(grads, counts, axes, direct):
    zero = jnp.zeros((COARSE, 2 * WIDTH), F32)
    own = zero
    for level in reversed(range(len(axes))):
        axis, bit = axes[level]
        side = lax.axis_index(axis) >> bit & 1
        wide = jnp.repeat(own, 2, axis=0)
        mine, theirs = ordered(side, wide[:COARSE], wide[COARSE:])
        if level >= direct:
            part = grads[level - direct].reshape(PACK, COARSE, HEAD_DIM).transpose(1, 0, 2)
            part = part.reshape(COARSE, 2 * WIDTH)
            theirs = theirs + part / jnp.maximum(counts[level - direct], 1.0)[:, None]
        own = mine + swapped(theirs, axis, bit)
    return own


def body(query_states, key_states, value_states, valid_mask, attended_grad):
    axes = level_axes()
    n_grp = lax.axis_size("grp")
    n_shard = lax.axis_size("shard")
    direct = min(DIRECT, len(axes))
    extra = len(axes) - direct
    operands = [
        query_states, key_states, value_states, valid_mask.reshape(1, TOK), attended_grad]
    grad_type = F32 if extra else BF
    outs = [jax.ShapeDtypeStruct((TOK, WIDTH), t) for t in (BF, BF, grad_type, grad_type)]
    if extra:
        tiles, counts = climb(key_states, value_states, valid_mask, axes, direct)
        operands.append(tiles)
        outs.append(jax.ShapeDtypeStruct((extra, TILE, HEAD_DIM), F32))
    vmem = pl.BlockSpec(memory_space=pltpu.VMEM)
    hbm = pl.BlockSpec(memory_space=pltpu.HBM)
    dma = pltpu.SemaphoreType.DMA
    all_rows = NEAR + (direct + extra) * COARSE
    results = pl.pallas_call(
        functools.partial(kernel, n_grp, n_shard, direct, extra),
        out_shape=outs,
        in_specs=[hbm] * 5 + [vmem] * (len(operands) - 5),
        out_specs=[hbm] * 4 + [vmem] * (len(outs) - 4),
        scratch_shapes=[
            pltpu.VMEM((TOK, WIDTH), BF),
            pltpu.VMEM((TOK, WIDTH), BF),
            pltpu.VMEM((TOK, WIDTH), grad_type),
            pltpu.VMEM((TOK, WIDTH), grad_type),
            dma((4,)),
            pltpu.VMEM((TOK, WIDTH), BF),
            pltpu.VMEM((TOK, WIDTH), BF),
            pltpu.VMEM((TOK, WIDTH), BF),
            pltpu.VMEM((TOK, WIDTH), BF),
            pltpu.VMEM((1, TOK), jnp.int32),
            dma((5,)),
            pltpu.VMEM((NEAR, WIDTH), BF),
            pltpu.VMEM((NEAR, WIDTH), BF),
            pltpu.VMEM((HALVES, up_offset(direct), HEAD_DIM), BF),
            pltpu.VMEM((direct * TILE, HEAD_DIM), BF),
            pltpu.VMEM((PACK, (direct + extra) * COARSE, HEAD_DIM), BF),
            pltpu.VMEM((128, HEAD_DIM), F32),
            pltpu.VMEM((PART_TILE, HEAD_DIM), F32),
            pltpu.VMEM((PART_TILE, HEAD_DIM), F32),
            pltpu.VMEM((all_rows, TOK), F32),
            pltpu.VMEM((HEADS, all_rows, TOK), F32),
            pltpu.VMEM((HEADS, all_rows, TOK), F32),
            pltpu.VMEM((all_rows, TOK), BF),
            pltpu.VMEM((all_rows, TOK), BF),
            pltpu.VMEM((TOK, 2 * WIDTH), F32),
            pltpu.VMEM((2, HALVES, BLOCK, WIDTH), BF),
            pltpu.VMEM((2, HALVES, BLOCK, WIDTH), BF),
            pltpu.VMEM((direct * TILE, HEAD_DIM), BF),
            pltpu.VMEM((direct * TILE, HEAD_DIM), BF),
            pltpu.VMEM((PACK, 128, HEAD_DIM), F32),
            dma((4 * HALVES,)),
            dma((4 * HALVES,)),
            dma((HALVES * direct,)),
            dma((HALVES * direct,)),
            dma((2 * HALVES,)),
            dma((2 * HALVES,)),
            dma((HALVES * direct,)),
            dma((HALVES * direct,)),
        ],
        compiler_params=pltpu.CompilerParams(
            collective_id=0, has_side_effects=True, vmem_limit_bytes=63 * 1024 * 1024
        ),
    )(*operands)
    if not extra:
        return pl.pallas_call(
            deliver,
            out_shape=outs,
            in_specs=[hbm] * 4,
            out_specs=[hbm] * 4,
            scratch_shapes=[pltpu.VMEM((4, TOK, WIDTH), BF), dma((4,)), dma((4,))],
            compiler_params=pltpu.CompilerParams(vmem_limit_bytes=63 * 1024 * 1024),
        )(*results)
    attended, query_grad, key_grad, value_grad, grads = results
    own = descend(grads, counts, axes, direct)
    spread = jnp.repeat(own, TOK // COARSE, axis=0) * valid_mask.astype(F32)[:, None]
    return (
        attended,
        query_grad,
        (key_grad + spread[:, :WIDTH]).astype(BF),
        (value_grad + spread[:, WIDTH:]).astype(BF),
    )


def solution(mesh):
    rows = P(("grp", "shard"), None)
    return jax.shard_map(
        body,
        mesh=mesh,
        in_specs=(rows, rows, rows, P(("grp", "shard")), rows),
        out_specs=(rows, rows, rows, rows),
        check_vma=False,
    )
```
